512 devices in a mesh: tm: 32 (over x_lo, z), tile: 8 (over y, core), plane: 2 (over x_hi).
Axes of the slice: x: 4 (x_hi: 2, x_lo: 2; x = x_hi * 2 + x_lo), y: 4, z: 16, core: 2. Of those that a mesh axis runs over, the one named last changes fastest.
Arguments:
- movie: bfloat16 [8, 8192, 8192], P(None, ('tile', 'plane'), 'tm'), may hold values from 0 to 1
- footprints: float32 [16, 8, 8192], P(None, None, ('tile', 'plane')), may hold values from 0 to 0.4
- traces: float32 [128, 8192], P(None, 'tm'), may hold values from 0 to 0.4
- patch_counts: int32 [8], replicated, may hold values from 1 to 16, 64 in all
- slot_neuron: int32 [128], replicated, may hold values from 0 to 127, each once
Outputs:
- new_footprints: float32 [16, 8, 8192], P(None, None, ('tile', 'plane'))
- new_traces: float32 [128, 8192], P(None, 'tm')
The draws below stay inside these ranges and needn't reach their ends.
Inputs may be any that keep to these rules, and one draw needn't show every extreme that they name: `patch_counts`: some patch holds exactly 16 neurons. `slot_neuron`: every neuron id stands exactly once.
All inputs are finite; a program needn't handle non-finite values.
Results may differ from the reference program's by a relative error of at most 0.0075.
Values sent between devices are 32-bit elements; how exact they have to be, the bound alone decides.
No kernel may reach another device: no remote copies, remote signals or barrier semaphores. Data moves between devices by JAX's collectives and lax.ppermute only.
A program may use at most 64 MiB of HBM per device.

```python
import math
import jax
import jax.numpy as jnp
import numpy as np
from jax import lax

PV = 8192
KP = 16
NPATCH = 8
ITERS = 2
SWEEPS = 3
FRAMES = 8192
NEURONS = 128


def block_scale(own_key, shape, pieces, smallest, top_value):
    factor_of = 1.0
    for dim, shards_of in pieces:
        heights = jax.random.uniform(jax.random.fold_in(jax.random.fold_in(own_key, 6), dim), (shards_of,), jnp.float32, smallest / len(pieces), top_value / len(pieces))
        factor_of = factor_of * jnp.repeat(jnp.exp(heights), shape[dim] // shards_of).reshape((-1,) + (1,) * (len(shape) - 1 - dim))
    return factor_of


def split_up(amount, total, most, slope):
    portions = [(1 << 20) // math.isqrt(grade ** slope) + 1 for grade in range(2, amount + 1)]
    surplus, holding = total - most - (amount - 1), [1] * (amount - 1)
    while surplus > 0:
        free = [i for i in range(amount - 1) if holding[i] < most]
        pool, left = sum([portions[i] for i in free]), surplus
        for i in free:
            extra = min(most - holding[i], max(1, left * portions[i] // pool), surplus)
            holding[i] = holding[i] + extra
            surplus = surplus - extra
    return np.array([most] + holding)


def ragged(key, count, total, bound, lean):
    if count == 2:
        one = jax.random.randint(key, (), max(1, total - bound), min(bound, total - 1) + 1)
        return jnp.stack([one, total - one])
    tallies = jnp.asarray(split_up(count, total, bound, lean), jnp.int32)
    twos = (count - 1) // 2
    giver, receiver = tallies[1:1 + 2 * twos:2], tallies[2:2 + 2 * twos:2]
    margin = jnp.minimum(giver - 1, bound - receiver)
    passed = jax.random.randint(jax.random.fold_in(key, 1), (twos,), 0, 1 << 20) % (margin + 1)
    tallies = tallies.at[1:1 + 2 * twos:2].set(giver - passed).at[2:2 + 2 * twos:2].set(receiver + passed)
    return tallies[jax.random.permutation(jax.random.fold_in(key, 2), count)]


def setup_inputs(seed: int = 0) -> dict:
    arg_keys = jax.random.split(jax.random.key(seed), 6)
    movie = jnp.clip(1.0 * jax.random.uniform(arg_keys[0], (NPATCH, PV, FRAMES), jnp.float32) ** block_scale(arg_keys[0], (NPATCH, PV, FRAMES), ((1, 16), (2, 32)), -0.2, 0.2), 0.0, 1.0).astype(jnp.bfloat16)
    footprints = jnp.clip(0.4 * jax.random.uniform(arg_keys[1], (KP, NPATCH, PV), jnp.float32) ** block_scale(arg_keys[1], (KP, NPATCH, PV), ((2, 16),), -0.2, 0.2), 0.0, 0.4)
    traces = jnp.clip(0.4 * jax.random.uniform(arg_keys[2], (NEURONS, FRAMES), jnp.float32) ** block_scale(arg_keys[2], (NEURONS, FRAMES), ((1, 32),), -0.2, 0.2), 0.0, 0.4)
    patch_counts = ragged(arg_keys[3], NPATCH, NPATCH * 8, KP, 1).astype(jnp.int32)
    slot_neuron = jax.random.permutation(arg_keys[4], NEURONS).astype(jnp.int32)
    return dict(movie=movie, footprints=footprints, traces=traces, patch_counts=patch_counts, slot_neuron=slot_neuron)


RIDGE = 1.0
HIGH = lax.Precision.HIGHEST


def hals_sweeps(values, target, gram):
    slot_count = values.shape[0]

    def advance(slot_index, current):
        gram_row = lax.dynamic_index_in_dim(gram, slot_index, 1, keepdims=False)
        mixed = jnp.einsum('pt,tpw->pw', gram_row, current, precision=HIGH)
        diagonal_term = lax.dynamic_index_in_dim(gram_row, slot_index, 1, keepdims=False)[:, None]
        own_value = lax.dynamic_index_in_dim(current, slot_index, 0, keepdims=False)
        target_row = lax.dynamic_index_in_dim(target, slot_index, 0, keepdims=False)
        refreshed = jnp.maximum((target_row - mixed + diagonal_term * own_value) / (diagonal_term + RIDGE), 0.0)
        return lax.dynamic_update_index_in_dim(current, refreshed, slot_index, 0)

    for sweep_index in range(SWEEPS):
        values = lax.fori_loop(0, slot_count, advance, values)
    return values


def project_patch(operands):
    weights, frames_block = operands
    return jnp.dot(weights, frames_block, preferred_element_type=jnp.float32)


def correlate_patch(operands):
    weights, frames_block = operands
    return lax.dot_general(weights, frames_block, (((1,), (1,)), ((), ())), preferred_element_type=jnp.float32)


def reference(movie, footprints, traces, patch_counts, slot_neuron):
    slot_count, patch_total, voxel_count = footprints.shape
    live = (jnp.arange(slot_count, dtype=jnp.int32)[:, None] < patch_counts[None, :]).astype(jnp.float32)
    shape_a = footprints * live[:, :, None]
    picked = traces[slot_neuron]
    shape_c = picked.reshape(patch_total, slot_count, -1).transpose(1, 0, 2) * live[:, :, None]
    for outer_index in range(ITERS):
        low_a = shape_a.astype(jnp.bfloat16)
        projected = lax.map(project_patch, (low_a.transpose(1, 0, 2), movie)).transpose(1, 0, 2)
        footprint_gram = jnp.einsum('spv,tpv->pst', shape_a, shape_a, precision=HIGH)
        shape_c = hals_sweeps(shape_c, projected, footprint_gram)
        low_c = shape_c.astype(jnp.bfloat16)
        correlated = lax.map(correlate_patch, (low_c.transpose(1, 0, 2), movie)).transpose(1, 0, 2)
        trace_gram = jnp.einsum('spf,tpf->pst', shape_c, shape_c, precision=HIGH)
        shape_a = hals_sweeps(shape_a, correlated, trace_gram)
    flat_c = shape_c.transpose(1, 0, 2).reshape(patch_total * slot_count, -1)
    flat_live = live.T.reshape(-1)
    kept = jnp.where(flat_live[:, None] > 0.5, flat_c, picked)
    new_traces = jnp.zeros_like(traces).at[slot_neuron].set(kept)
    return shape_a, new_traces
```

```python
import functools

import jax
import jax.numpy as jnp
from jax import lax
from jax.experimental import pallas as pl
from jax.experimental.pallas import tpu as pltpu
from jax.sharding import PartitionSpec as P

ITERS = 2
SWEEPS = 3
RIDGE = 1.0
HIGH = lax.Precision.HIGHEST
F32 = jnp.float32
BF16 = jnp.bfloat16
KP = 16
NP = 8
LIVE = 64
VOX = ("tile", "plane")

SMEM = pl.BlockSpec(memory_space=pltpu.SMEM)
VMEM = pl.BlockSpec(memory_space=pltpu.VMEM)


def nn(a, b, **kw):
    return lax.dot_general(a, b, (((1,), (0,)), ((), ())), preferred_element_type=F32, **kw)


def nt(a, b, **kw):
    return lax.dot_general(a, b, (((1,), (1,)), ((), ())), preferred_element_type=F32, **kw)


def offsets(counts):
    offs = [jnp.int32(0)]
    for p in range(NP):
        offs.append(offs[-1] + counts[p])
    return offs


def iota(shape, dim):
    return lax.broadcasted_iota(jnp.int32, shape, dim)


def patch_and_slot(counts, shape, dim):
    offs = offsets(counts)
    r = iota(shape, dim)
    patch = jnp.zeros(shape, jnp.int32)
    slot = r
    for p in range(1, NP):
        at = r >= offs[p]
        patch = jnp.where(at, p, patch)
        slot = jnp.where(at, r - offs[p], slot)
    return patch, slot


def unpacker(counts):
    offs = offsets(counts)
    shape = (KP * NP, LIVE)
    q, r = iota(shape, 0), iota(shape, 1)
    p, s = q % NP, q // NP
    off = jnp.zeros(shape, jnp.int32)
    cnt = jnp.zeros(shape, jnp.int32)
    for i in range(NP):
        off = jnp.where(p == i, offs[i], off)
        cnt = jnp.where(p == i, counts[i], cnt)
    return ((r == off + s) & (s < cnt)).astype(F32)


def packer(counts):
    shape = (LIVE, KP * NP)
    patch, slot = patch_and_slot(counts, shape, 0)
    return (iota(shape, 1) == slot * NP + patch).astype(F32)


def gram_chunk(counts, full):
    shape = (LIVE, LIVE)
    patch_a, _ = patch_and_slot(counts, shape, 0)
    patch_b, _ = patch_and_slot(counts, shape, 1)
    own = jnp.where(patch_a == patch_b, full, 0.0)
    _, slot = patch_and_slot(counts, (KP, LIVE), 1)
    pick = (slot == iota((KP, LIVE), 0)).astype(F32)
    by_slot = nn(pick, own, precision=HIGH)
    return jnp.concatenate([by_slot[:8], by_slot[8:]], axis=1)


def project_packed(counts, packed, movie_ref, send_ref):
    low = packed.astype(BF16)
    patch, _ = patch_and_slot(counts, low.shape, 0)
    zero = jnp.zeros_like(low)
    total = jnp.zeros((LIVE, movie_ref.shape[2]), F32)
    for p in range(NP):
        total += nn(jnp.where(patch == p, low, zero), movie_ref[p])
    gram = gram_chunk(counts, nt(packed, packed, precision=HIGH))
    stacked = jnp.concatenate([total[:, :128], total[:, 128:]], axis=0)
    chunks = stacked.T
    for j in range(send_ref.shape[0]):
        send_ref[j, 0:8, :] = chunks[8 * j : 8 * j + 8]
        send_ref[j, 8:16, :] = gram


def first_project_kernel(counts, foot_ref, movie_ref, send_ref):
    packed = nn(packer(counts), foot_ref[...], precision=HIGH)
    project_packed(counts, packed, movie_ref, send_ref)


def project_kernel(counts, gathered_ref, movie_ref, send_ref):
    rows = jnp.concatenate([gathered_ref[:128].T, gathered_ref[128:].T], axis=1)
    packed = jnp.concatenate([rows[:LIVE], rows[LIVE:]], axis=1)
    project_packed(counts, packed, movie_ref, send_ref)


def correlate_kernel(counts, gathered_ref, movie_ref, send_ref):
    by_frame = gathered_ref[...]
    rows = by_frame.T
    cols = jnp.concatenate([by_frame[:, :LIVE], by_frame[:, LIVE:]], axis=0)
    gram = gram_chunk(
        counts,
        nt(rows[:LIVE], rows[:LIVE], precision=HIGH) + nt(rows[LIVE:], rows[LIVE:], precision=HIGH),
    )
    low = cols.astype(BF16)
    patch, _ = patch_and_slot(counts, low.shape, 1)
    zero = jnp.zeros_like(low)
    total = jnp.zeros((movie_ref.shape[1], LIVE), F32)
    for p in range(NP):
        total += nn(movie_ref[p], jnp.where(patch == p, low, zero))
    half = total.shape[0] // 2
    chunks = jnp.concatenate([total[:half], total[half:]], axis=1)
    for i in range(send_ref.shape[0]):
        send_ref[i, 0:8, :] = chunks[8 * i : 8 * i + 8]
        send_ref[i, 8:16, :] = gram


def own_columns(ref, index, lanes):
    base = pl.multiple_of((index // 16) * 128, 128)
    turn = 8 * (index % 16)
    low = pltpu.roll(ref[:, pl.ds(base, 128)], (128 - turn) % 128, 1)
    high = pltpu.roll(ref[:, pl.ds(lanes + base, 128)], (136 - turn) % 128, 1)
    return jnp.where(iota(low.shape, 1) < 8, low, high)


def start_kernel(counts, where, foot_ref, traces_ref, choose_ref, first_c_ref, first_a_ref):
    q = iota((KP * NP, 128), 0)
    cnt = jnp.zeros(q.shape, jnp.int32)
    for p in range(NP):
        cnt = jnp.where(q % NP == p, counts[p], cnt)
    live = q // NP < cnt
    keep = live & (iota(q.shape, 1) < 16)
    first_a = own_columns(foot_ref, where[0], foot_ref.shape[1] // 2)
    first_a_ref[...] = jnp.where(keep, first_a, 0.0)
    traces = own_columns(traces_ref, where[1], traces_ref.shape[1] // 2)
    first_c_ref[...] = jnp.where(keep, nn(choose_ref[...], traces, precision=HIGH), 0.0)


def hals_kernel(counts, got_ref, x_ref, send_ref, new_ref, rows, wide):
    n = got_ref.shape[0]
    parts = [got_ref[j] for j in range(n)]
    while len(parts) > 1:
        parts = [a + b for a, b in zip(parts[::2], parts[1::2])]
    total = parts[0]
    cols = jnp.concatenate([total[:, :LIVE], total[:, LIVE:]], axis=0)
    order = jnp.concatenate([cols[0:8], cols[16:24], cols[8:16], cols[24:32]], axis=0)
    unpack = unpacker(counts)
    rows[:, 0:32] = nt(unpack, order, precision=HIGH)
    shape = (NP, 128)
    scale = []
    for k in range(KP):
        own = rows[8 * k : 8 * k + 8, :]
        for t in range(KP):
            entry = jnp.broadcast_to(own[:, 16 + t : 17 + t], shape)
            if t == k:
                scale.append(1.0 / (entry + RIDGE))
            wide[KP * k + t] = entry
    for k in range(KP):
        wide[KP * k + k] = scale[k]

    def sweep(_, xs):
        xs = list(xs)
        for k in range(KP):
            terms = [wide[KP * k + t] * xs[t] for t in range(KP) if t != k]
            last = terms.pop(k - 1 if k else KP - 2)
            while len(terms) > 1:
                odd = [terms[-1]] if len(terms) % 2 else []
                terms = [a + b for a, b in zip(terms[::2], terms[1::2])] + odd
            rest = rows[8 * k : 8 * k + 8, :] - terms[0]
            xs[k] = jnp.maximum((rest - last) * wide[KP * k + k], 0.0)
        return tuple(xs)

    keep = iota(shape, 1) < 16
    xs = lax.fori_loop(0, SWEEPS, sweep, tuple(x_ref[8 * k : 8 * k + 8, :] for k in range(KP)))
    for k in range(KP):
        new_ref[8 * k : 8 * k + 8, :] = jnp.where(keep, xs[k], 0.0)
    by_col = new_ref[...].T[:16]
    packed = nn(by_col, unpack, precision=HIGH)
    chunk = jnp.concatenate([packed[:8], packed[8:]], axis=1)
    for j in range(n):
        send_ref[j] = chunk


def footprints_kernel(counts, gathered_ref, out_ref):
    half = gathered_ref.shape[0]
    unpack = unpacker(counts)
    gathered = gathered_ref[...]
    out_ref[:, :half] = nt(unpack, gathered[:, :LIVE], precision=HIGH)
    out_ref[:, half:] = nt(unpack, gathered[:, LIVE:], precision=HIGH)


def traces_kernel(counts, gathered_ref, traces_ref, home_ref, out_ref):
    half = gathered_ref.shape[0]
    gathered = gathered_ref[...]
    home = home_ref[...]
    place = nn(home, unpacker(counts), precision=HIGH)
    live = jnp.sum(home, axis=1, keepdims=True) > 0.5
    for h in range(2):
        at = slice(half * h, half * h + half)
        moved = nt(place, gathered[:, LIVE * h : LIVE * h + LIVE], precision=HIGH)
        out_ref[:, at] = jnp.where(live, moved, traces_ref[:, at])


def call(kernel, outs, smem, args, scratch=()):
    return pl.pallas_call(
        kernel,
        out_shape=[jax.ShapeDtypeStruct(s, F32) for s in outs],
        in_specs=[SMEM] * smem + [VMEM] * (len(args) - smem),
        out_specs=[VMEM] * len(outs),
        scratch_shapes=list(scratch),
        compiler_params=pltpu.CompilerParams(vmem_limit_bytes=32 * 1024 * 1024),
    )(*args)


def local(n_tm, n_vox, movie, footprints, traces, patch_counts, slot_neuron):
    slots, patches, voxels = footprints.shape
    frames = movie.shape[2]
    q = slots * patches
    foot = footprints.reshape(q, voxels)
    neuron = slot_neuron.reshape(patches, slots).T.reshape(q)
    live = (jnp.arange(slots, dtype=jnp.int32)[:, None] < patch_counts[None, :]).reshape(q)
    ids = jnp.arange(q, dtype=jnp.int32)
    choose = ((neuron[:, None] == ids[None, :]) & live[:, None]).astype(F32)
    home = ((neuron[None, :] == ids[:, None]) & live[None, :]).astype(F32)
    where = jnp.stack([lax.axis_index("tm"), lax.axis_index(VOX)]).astype(jnp.int32)

    def swap(x, axes):
        return lax.all_to_all(x, axes, 0, 0, tiled=True)

    def hals(n, got, x):
        scratch = [pltpu.VMEM((q, 128), F32), pltpu.VMEM((KP * KP, NP, 128), F32)]
        return call(hals_kernel, [(n, 8, 128), (q, 128)], 1, [patch_counts, got, x], scratch)

    chunk_c = (n_vox, 16, 128)
    chunk_a = (n_tm, 16, 128)
    x_c, x_a = call(start_kernel, [(q, 128)] * 2, 2, [patch_counts, where, foot, traces, choose])
    for step in range(ITERS):
        if step == 0:
            (send,) = call(first_project_kernel, [chunk_c], 1, [patch_counts, foot, movie])
        else:
            (send,) = call(project_kernel, [chunk_c], 1, [patch_counts, all_a, movie])
        send, x_c = hals(n_vox, swap(send, VOX), x_c)
        all_c = swap(send, VOX).reshape(frames // 2, 128)
        (send,) = call(correlate_kernel, [chunk_a], 1, [patch_counts, all_c, movie])
        send, x_a = hals(n_tm, swap(send, "tm"), x_a)
        all_a = swap(send, "tm").reshape(voxels // 2, 128)
    (new_traces,) = call(traces_kernel, [traces.shape], 1, [patch_counts, all_c, traces, home])
    (new_foot,) = call(footprints_kernel, [foot.shape], 1, [patch_counts, all_a])
    return new_foot.reshape(footprints.shape), new_traces


def solution(mesh):
    placed = (
        P(None, ("tile", "plane"), "tm"),
        P(None, None, ("tile", "plane")),
        P(None, "tm"),
        P(),
        P(),
    )
    n_tm = mesh.shape["tm"]
    n_vox = mesh.shape["tile"] * mesh.shape["plane"]
    return jax.shard_map(
        functools.partial(local, n_tm, n_vox),
        mesh=mesh,
        in_specs=placed,
        out_specs=(P(None, None, ("tile", "plane")), P(None, "tm")),
        check_vma=False,
    )
```

```python
import functools

import jax
import jax.numpy as jnp
from jax import lax
from jax.experimental import pallas as pl
from jax.experimental.pallas import tpu as pltpu
from jax.sharding import PartitionSpec as P

ITERS = 2
SWEEPS = 3
RIDGE = 1.0
HIGH = lax.Precision.HIGHEST
F32 = jnp.float32
BF16 = jnp.bfloat16
KP = 16
NP = 8
LIVE = 64
ACROSS = ("y", "plane")
NEAR = ("x", "zn")
FAR = "zf"
GRAM = 8

SMEM = pl.BlockSpec(memory_space=pltpu.SMEM)
VMEM = pl.BlockSpec(memory_space=pltpu.VMEM)
HBM = pl.BlockSpec(memory_space=pltpu.HBM)


def nn(a, b, **kw):
    return lax.dot_general(a, b, (((1,), (0,)), ((), ())), preferred_element_type=F32, **kw)


def nt(a, b, **kw):
    return lax.dot_general(a, b, (((1,), (1,)), ((), ())), preferred_element_type=F32, **kw)


def offsets(counts):
    offs = [jnp.int32(0)]
    for p in range(NP):
        offs.append(offs[-1] + counts[p])
    return offs


def iota(shape, dim):
    return lax.broadcasted_iota(jnp.int32, shape, dim)


def patch_and_slot(counts, shape, dim):
    offs = offsets(counts)
    r = iota(shape, dim)
    patch = jnp.zeros(shape, jnp.int32)
    slot = r
    for p in range(1, NP):
        at = r >= offs[p]
        patch = jnp.where(at, p, patch)
        slot = jnp.where(at, r - offs[p], slot)
    return patch, slot


def unpacker(counts):
    offs = offsets(counts)
    shape = (KP * NP, LIVE)
    q, r = iota(shape, 0), iota(shape, 1)
    p, s = q % NP, q // NP
    off = jnp.zeros(shape, jnp.int32)
    cnt = jnp.zeros(shape, jnp.int32)
    for i in range(NP):
        off = jnp.where(p == i, offs[i], off)
        cnt = jnp.where(p == i, counts[i], cnt)
    return ((r == off + s) & (s < cnt)).astype(F32)


def packer(counts):
    shape = (LIVE, KP * NP)
    patch, slot = patch_and_slot(counts, shape, 0)
    return (iota(shape, 1) == slot * NP + patch).astype(F32)


def gram_chunk(counts, full):
    shape = (LIVE, LIVE)
    patch_a, _ = patch_and_slot(counts, shape, 0)
    patch_b, _ = patch_and_slot(counts, shape, 1)
    own = jnp.where(patch_a == patch_b, full, 0.0)
    _, slot = patch_and_slot(counts, (KP, LIVE), 1)
    pick = (slot == iota((KP, LIVE), 0)).astype(F32)
    by_slot = nn(pick, own, precision=HIGH)
    return jnp.concatenate([by_slot[:8], by_slot[8:]], axis=1)


def project_packed(counts, packed, movie, out_ref):
    low = packed.astype(BF16)
    patch, _ = patch_and_slot(counts, low.shape, 0)
    zero = jnp.zeros_like(low)
    total = None
    for p in range(NP):
        term = nn(jnp.where(patch == p, low, zero), movie(p))
        total = term if p == 0 else total + term
    gram = gram_chunk(counts, nt(packed, packed, precision=HIGH))
    for h in range(2):
        out_ref[h, :LIVE, :] = total[:, 128 * h : 128 * h + 128]
        out_ref[h, LIVE:, :] = gram


def first_project_kernel(counts, foot_ref, movie_ref, out_ref, movie_buf, foot_buf, sems):
    copies = [pltpu.make_async_copy(foot_ref, foot_buf, sems.at[NP])]
    for p in range(NP):
        copies.append(pltpu.make_async_copy(movie_ref.at[p], movie_buf.at[p], sems.at[p]))
    for copy in copies:
        copy.start()
    copies[0].wait()
    packed = nn(packer(counts), foot_buf[...], precision=HIGH)

    def movie(p):
        copies[p + 1].wait()
        return movie_buf[p]

    project_packed(counts, packed, movie, out_ref)


def project_kernel(counts, gathered_ref, movie_ref, out_ref):
    rows = jnp.concatenate([gathered_ref[:128].T, gathered_ref[128:].T], axis=1)
    packed = jnp.concatenate([rows[:LIVE], rows[LIVE:]], axis=1)
    project_packed(counts, packed, lambda p: movie_ref[p], out_ref)


def keep_half_kernel(where, got_ref, send_ref):
    kept = got_ref[0, where[0]] + got_ref[1, where[0]]
    for j in range(send_ref.shape[0]):
        send_ref[j] = kept


def keep_part_kernel(got_ref, send_ref):
    total = tree_sum([got_ref[j] for j in range(got_ref.shape[0])])
    for j in range(send_ref.shape[0]):
        send_ref[j] = total


def correlate_kernel(counts, gathered_ref, movie_ref, send_ref):
    rows = jnp.concatenate([gathered_ref[0], gathered_ref[1]], axis=1)
    gram = gram_chunk(counts, nt(rows, rows, precision=HIGH))
    low = rows.T.astype(BF16)
    patch, _ = patch_and_slot(counts, low.shape, 1)
    zero = jnp.zeros_like(low)
    total = None
    for p in range(NP):
        term = nn(movie_ref[p], jnp.where(patch == p, low, zero))
        total = term if p == 0 else total + term
    half = total.shape[0] // 2
    chunks = jnp.concatenate([total[:half], total[half:]], axis=1)
    n = send_ref.shape[0]
    size = half // n
    for i in range(n):
        send_ref[i, :size, :] = chunks[size * i : size * i + size]
        send_ref[i, size:, :] = gram


def start_kernel(counts, where, foot_ref, traces_ref, choose_ref, first_c_ref, first_a_ref):
    q = iota((KP * NP, 128), 0)
    lane = iota(q.shape, 1)
    cnt = jnp.zeros(q.shape, jnp.int32)
    for p in range(NP):
        cnt = jnp.where(q % NP == p, counts[p], cnt)
    half = foot_ref.shape[1] // 2
    base = pl.multiple_of((where[1] // 4) * 128, 128)
    turn = 32 * (where[1] % 4)
    first = pltpu.roll(foot_ref[:, pl.ds(base, 128)], (128 - turn) % 128, 1)
    second = pltpu.roll(foot_ref[:, pl.ds(half + base, 128)], (160 - turn) % 128, 1)
    own = jnp.where(lane < 32, first, second)
    first_a_ref[...] = jnp.where((q // NP < cnt) & (lane < 64), own, 0.0)
    traces = traces_ref[:, pl.ds(pl.multiple_of(where[0] * 128, 128), 128)]
    first_c_ref[...] = nn(choose_ref[...], traces, precision=HIGH)


def tree_sum(parts):
    while len(parts) > 1:
        odd = [parts[-1]] if len(parts) % 2 else []
        parts = [a + b for a, b in zip(parts[::2], parts[1::2])] + odd
    return parts[0]


def hals(target, gram, x_ref, new_ref, wide):
    shape = (NP, 128)
    for k in range(KP):
        own = gram(k)
        for t in range(KP):
            entry = jnp.broadcast_to(own[:, t : t + 1], shape)
            wide[KP * k + t] = 1.0 / (entry + RIDGE) if t == k else entry

    def sweep(_, xs):
        xs = list(xs)
        for k in range(KP):
            terms = [wide[KP * k + t] * xs[t] for t in range(KP) if t != k]
            last = terms.pop(k - 1 if k else KP - 2)
            rest = target(k) - tree_sum(terms)
            xs[k] = jnp.maximum((rest - last) * wide[KP * k + k], 0.0)
        return tuple(xs)

    xs = lax.fori_loop(0, SWEEPS, sweep, tuple(x_ref[8 * k : 8 * k + 8, :] for k in range(KP)))
    for k in range(KP):
        new_ref[8 * k : 8 * k + 8, :] = xs[k]


def hals_traces_kernel(counts, got_ref, x_ref, out_ref, new_ref, rows, grams, wide):
    total = tree_sum([got_ref[j] for j in range(got_ref.shape[0])])
    unpack = unpacker(counts)
    gram = total[LIVE:]
    gram = jnp.concatenate([gram[:, :LIVE], gram[:, LIVE:]], axis=0)
    rows[...] = nn(unpack, total[:LIVE], precision=HIGH)
    grams[:, :KP] = nt(unpack, gram, precision=HIGH)
    hals(lambda k: rows[8 * k : 8 * k + 8, :], lambda k: grams[8 * k : 8 * k + 8, :KP], x_ref, new_ref, wide)
    out_ref[...] = nn(packer(counts), new_ref[...], precision=HIGH)


def hals_footprints_kernel(counts, got_ref, x_ref, send_ref, new_ref, rows, grams, wide):
    total = tree_sum([got_ref[j] for j in range(got_ref.shape[0])])
    unpack = unpacker(counts)
    size = total.shape[0] - GRAM
    cols = jnp.concatenate([total[:size, :LIVE], total[:size, LIVE:]], axis=0)
    gram = total[size:]
    gram = jnp.concatenate([gram[:, :LIVE], gram[:, LIVE:]], axis=0)
    rows[:, : 2 * size] = nt(unpack, cols, precision=HIGH)
    rows[:, 2 * size :] = jnp.zeros((KP * NP, 128 - 2 * size), F32)
    grams[:, :KP] = nt(unpack, gram, precision=HIGH)
    hals(lambda k: rows[8 * k : 8 * k + 8, :], lambda k: grams[8 * k : 8 * k + 8, :KP], x_ref, new_ref, wide)
    packed = nn(new_ref[...].T[: 2 * size], unpack, precision=HIGH)
    chunk = jnp.concatenate([packed[:size], packed[size:]], axis=1)
    for j in range(send_ref.shape[0]):
        send_ref[j] = chunk


def footprints_kernel(counts, gathered_ref, out_ref):
    half = gathered_ref.shape[0]
    unpack = unpacker(counts)
    gathered = gathered_ref[...]
    out_ref[:, :half] = nt(unpack, gathered[:, :LIVE], precision=HIGH)
    out_ref[:, half:] = nt(unpack, gathered[:, LIVE:], precision=HIGH)


def traces_kernel(counts, gathered_ref, traces_ref, home_ref, out_ref):
    home = home_ref[...]
    place = nn(home, unpacker(counts), precision=HIGH)
    live = jnp.sum(home, axis=1, keepdims=True) > 0.5
    for h in range(2):
        at = slice(128 * h, 128 * h + 128)
        moved = nn(place, gathered_ref[h], precision=HIGH)
        out_ref[:, at] = jnp.where(live, moved, traces_ref[:, at])


def call(kernel, outs, specs, args, scratch=()):
    return pl.pallas_call(
        kernel,
        out_shape=[jax.ShapeDtypeStruct(s, F32) for s in outs],
        in_specs=specs + [VMEM] * (len(args) - len(specs)),
        out_specs=[VMEM] * len(outs),
        scratch_shapes=list(scratch),
        compiler_params=pltpu.CompilerParams(vmem_limit_bytes=32 * 1024 * 1024),
    )(*args)


def local(sizes, movie, footprints, traces, patch_counts, slot_neuron):
    n_across, n_near, n_far = sizes
    slots, patches, voxels = footprints.shape
    q = slots * patches
    foot = footprints.reshape(q, voxels)
    neuron = slot_neuron.reshape(patches, slots).T.reshape(q)
    live = (jnp.arange(slots, dtype=jnp.int32)[:, None] < patch_counts[None, :]).reshape(q)
    ids = jnp.arange(q, dtype=jnp.int32)
    choose = ((neuron[:, None] == ids[None, :]) & live[:, None]).astype(F32)
    home = ((neuron[None, :] == ids[:, None]) & live[None, :]).astype(F32)
    where = jnp.stack([lax.axis_index("core"), lax.axis_index(NEAR)]).astype(jnp.int32)

    def swap(x, axes):
        return lax.all_to_all(x, axes, 0, 0, tiled=True)

    def cores(x):
        return lax.all_gather(x, "core", axis=0, tiled=False)

    scratch = [pltpu.VMEM((q, 128), F32), pltpu.VMEM((q, 128), F32), pltpu.VMEM((KP * KP, NP, 128), F32)]
    part = voxels // 2 // n_near
    x_c, x_a = call(start_kernel, [(q, 128)] * 2, [SMEM] * 2, [patch_counts, where, foot, traces, choose])
    for step in range(ITERS):
        halves = [(2, LIVE + GRAM, 128)]
        if step == 0:
            buffers = [
                pltpu.VMEM(movie.shape, movie.dtype),
                pltpu.VMEM(foot.shape, F32),
                pltpu.SemaphoreType.DMA((NP + 1,)),
            ]
            specs = [SMEM, HBM, HBM]
            (partial,) = call(first_project_kernel, halves, specs, [patch_counts, foot, movie], buffers)
        else:
            (partial,) = call(project_kernel, halves, [SMEM], [patch_counts, all_a, movie])
        (send,) = call(keep_half_kernel, [(n_across, LIVE + GRAM, 128)], [SMEM], [where, cores(partial)])
        own_c, x_c = call(
            hals_traces_kernel, [(LIVE, 128), (q, 128)], [SMEM], [patch_counts, swap(send, ACROSS), x_c], scratch
        )
        all_c = cores(own_c)
        (send,) = call(correlate_kernel, [(n_near, part + GRAM, 128)], [SMEM], [patch_counts, all_c, movie])
        (send,) = call(keep_part_kernel, [(n_far, part + GRAM, 128)], [], [swap(send, NEAR)])
        send, x_a = call(
            hals_footprints_kernel,
            [(n_near, part, 128), (q, 128)],
            [SMEM],
            [patch_counts, swap(send, FAR), x_a],
            scratch,
        )
        all_a = swap(send, NEAR).reshape(voxels // 2, 128)
    (new_traces,) = call(traces_kernel, [traces.shape], [SMEM], [patch_counts, all_c, traces, home])
    (new_foot,) = call(footprints_kernel, [foot.shape], [SMEM], [patch_counts, all_a])
    return new_foot.reshape(footprints.shape), new_traces


def solution(mesh):
    names = ("x", "zf", "zn", "y", "core", "plane")
    shape = (2, mesh.shape["tm"] // 8, 4, mesh.shape["tile"] // 2, 2, mesh.shape["plane"])
    fine = jax.sharding.Mesh(mesh.devices.reshape(shape), names)
    frames, voxels = names[:3], names[3:]
    sizes = (shape[3] * shape[5], shape[0] * shape[2], shape[1])
    return jax.shard_map(
        functools.partial(local, sizes),
        mesh=fine,
        in_specs=(P(None, voxels, frames), P(None, None, voxels), P(None, frames), P(), P()),
        out_specs=(P(None, None, voxels), P(None, frames)),
        check_vma=False,
    )
```

```python
import functools

import jax
import jax.numpy as jnp
from jax import lax
from jax.experimental import pallas as pl
from jax.experimental.pallas import tpu as pltpu
from jax.sharding import PartitionSpec as P

ITERS = 2
SWEEPS = 3
RIDGE = 1.0
HIGH = lax.Precision.HIGHEST
F32 = jnp.float32
BF16 = jnp.bfloat16
KP = 16
NP = 8
LIVE = 64
ACROSS = ("y", "plane")
NEAR = ("x", "zn")
FAR = "zf"
GRAM = 8

VMEM = pl.BlockSpec(memory_space=pltpu.VMEM)
HBM = pl.BlockSpec(memory_space=pltpu.HBM)


def nn(a, b, **kw):
    return lax.dot_general(a, b, (((1,), (0,)), ((), ())), preferred_element_type=F32, **kw)


def nt(a, b, **kw):
    return lax.dot_general(a, b, (((1,), (1,)), ((), ())), preferred_element_type=F32, **kw)


def split(x):
    high = x.astype(BF16)
    rest = x - high.astype(F32)
    middle = rest.astype(BF16)
    return [high, middle, (rest - middle.astype(F32)).astype(BF16)]


def choose_rows(pick, x):
    return nn(jnp.concatenate([pick.astype(BF16)] * 3, axis=1), jnp.concatenate(split(x), axis=0))


def choose_cols(pick, x):
    return nt(jnp.concatenate([pick.astype(BF16)] * 3, axis=1), jnp.concatenate(split(x), axis=1))


def spread(counts_ref):
    return [jnp.broadcast_to(counts_ref[:, p : p + 1], (1, 128)) for p in range(NP)]


def fit(row, shape):
    return row[:, : shape[1]] if shape[1] <= 128 else jnp.concatenate([row] * (shape[1] // 128), axis=1)


def offsets(counts, shape):
    offs = [jnp.zeros((1, 128), jnp.int32)]
    for p in range(NP - 1):
        offs.append(offs[-1] + counts[p])
    return [fit(off, shape) for off in offs]


def iota(shape, dim):
    return lax.broadcasted_iota(jnp.int32, shape, dim)


def patch_and_slot(counts, shape, dim):
    offs = offsets(counts, shape)
    r = iota(shape, dim)
    patch = jnp.zeros(shape, jnp.int32)
    slot = r
    for p in range(1, NP):
        at = r >= offs[p]
        patch = jnp.where(at, p, patch)
        slot = jnp.where(at, r - offs[p], slot)
    return patch, slot


def unpacker(counts):
    shape = (NP, LIVE)
    offs = offsets(counts, shape)
    p, r = iota(shape, 0), iota(shape, 1)
    off = jnp.zeros(shape, jnp.int32)
    cnt = jnp.zeros(shape, jnp.int32)
    for i in range(NP):
        off = jnp.where(p == i, offs[i], off)
        cnt = jnp.where(p == i, fit(counts[i], shape), cnt)
    return jnp.concatenate([((r == off + s) & (s < cnt)).astype(F32) for s in range(KP)], axis=0)


def packer(counts):
    shape = (LIVE, KP * NP)
    patch, slot = patch_and_slot(counts, shape, 0)
    return (iota(shape, 1) == slot * NP + patch).astype(F32)


def gram_chunk(counts, full):
    shape = (LIVE, LIVE)
    patch_a, _ = patch_and_slot(counts, shape, 0)
    patch_b, _ = patch_and_slot(counts, shape, 1)
    own = jnp.where(patch_a == patch_b, full, 0.0)
    _, slot = patch_and_slot(counts, (KP, LIVE), 1)
    pick = (slot == iota((KP, LIVE), 0)).astype(F32)
    by_slot = choose_rows(pick, own)
    return jnp.concatenate([by_slot[:8], by_slot[8:]], axis=1)


def project_packed(counts, packed, movie, out_ref):
    low = packed.astype(BF16)
    patch, _ = patch_and_slot(counts, low.shape, 0)
    zero = jnp.zeros_like(low)
    total = None
    for p in range(NP):
        term = nn(jnp.where(patch == p, low, zero), movie(p))
        total = term if p == 0 else total + term
    gram = gram_chunk(counts, nt(packed, packed, precision=HIGH))
    for h in range(2):
        out_ref[h, :LIVE, :] = total[:, 128 * h : 128 * h + 128]
        out_ref[h, LIVE:, :] = gram


def neuron_slots(neuron):
    shape = (KP * NP, KP * NP)
    return (iota(shape, 0) == neuron).astype(BF16)


def first_columns(counts, neuron, foot_ref, traces, first_c_ref, first_a_ref):
    shape = (KP * NP, KP * NP)
    q, lane = iota(shape, 0), iota(shape, 1)
    cnt = jnp.zeros(shape, jnp.int32)
    for p in range(NP):
        cnt = jnp.where(q % NP == p, counts[p], cnt)
    live = q // NP < cnt
    half = foot_ref.shape[1] // 2
    near = lax.axis_index(NEAR)
    base = pl.multiple_of((near // 4) * 128, 128)
    turn = 32 * (near % 4)
    first = pltpu.roll(foot_ref[:, pl.ds(base, 128)], (128 - turn) % 128, 1)
    second = pltpu.roll(foot_ref[:, pl.ds(half + base, 128)], (160 - turn) % 128, 1)
    own = jnp.where(lane < 32, first, second)
    first_a_ref[...] = jnp.where(live & (lane < 64), own, 0.0)
    order = (lane == (q % NP) * KP + q // NP).astype(BF16)
    choose = nt(order, neuron_slots(neuron))
    first_c_ref[...] = jnp.where(live, choose_rows(choose, traces), 0.0)


def first_kernel(counts_hbm, neuron_hbm, foot_hbm, traces_hbm, movie_hbm, *refs):
    out_ref, first_c_ref, first_a_ref, counts_ref, neuron_ref, foot_ref, traces_ref, movie_ref, sems = refs
    half = traces_ref.shape[1]
    own = pl.ds(pl.multiple_of(lax.axis_index("core") * half, half), half)
    pairs = [
        (counts_hbm, counts_ref),
        (neuron_hbm, neuron_ref),
        (foot_hbm, foot_ref),
        (traces_hbm.at[:, own], traces_ref),
    ]
    pairs += [(movie_hbm.at[p], movie_ref.at[p]) for p in range(NP)]
    copies = [pltpu.make_async_copy(src, dst, sems.at[i]) for i, (src, dst) in enumerate(pairs)]
    for copy in copies:
        copy.start()
    for copy in copies[:4]:
        copy.wait()
    counts = spread(counts_ref)
    packed = choose_rows(packer(counts), foot_ref[...])

    def movie(p):
        copies[4 + p].wait()
        return movie_ref[p]

    project_packed(counts, packed, movie, out_ref)
    first_columns(counts, neuron_ref[...], foot_ref, traces_ref[...], first_c_ref, first_a_ref)


def project_kernel(counts_ref, gathered_ref, movie_ref, out_ref):
    counts = spread(counts_ref)
    rows = jnp.concatenate([gathered_ref[:128].T, gathered_ref[128:].T], axis=1)
    packed = jnp.concatenate([rows[:LIVE], rows[LIVE:]], axis=1)
    project_packed(counts, packed, lambda p: movie_ref[p], out_ref)


def keep_half_kernel(got_ref, send_ref):
    core = lax.axis_index("core")
    kept = got_ref[0, core] + got_ref[1, core]
    for j in range(send_ref.shape[0]):
        send_ref[j] = kept


def keep_part_kernel(got_ref, send_ref):
    total = tree_sum([got_ref[j] for j in range(got_ref.shape[0])])
    for j in range(send_ref.shape[0]):
        send_ref[j] = total


def correlate_kernel(counts_ref, gathered_ref, movie_ref, send_ref):
    counts = spread(counts_ref)
    rows = jnp.concatenate([gathered_ref[0], gathered_ref[1]], axis=1)
    gram = gram_chunk(counts, nt(rows, rows, precision=HIGH))
    low = rows.T.astype(BF16)
    patch, _ = patch_and_slot(counts, low.shape, 1)
    zero = jnp.zeros_like(low)
    total = None
    for p in range(NP):
        term = nn(movie_ref[p], jnp.where(patch == p, low, zero))
        total = term if p == 0 else total + term
    half = total.shape[0] // 2
    chunks = jnp.concatenate([total[:half], total[half:]], axis=1)
    n = send_ref.shape[0]
    size = half // n
    for i in range(n):
        send_ref[i, :size, :] = chunks[size * i : size * i + size]
        send_ref[i, size:, :] = gram


def tree_sum(parts):
    while len(parts) > 1:
        odd = [parts[-1]] if len(parts) % 2 else []
        parts = [a + b for a, b in zip(parts[::2], parts[1::2])] + odd
    return parts[0]


def hals(target, gram, x_ref, new_ref, wide):
    shape = (NP, 128)
    for k in range(KP):
        own = gram(k)
        scale = 1.0 / (jnp.broadcast_to(own[:, k : k + 1], shape) + RIDGE)
        for t in range(KP):
            entry = jnp.broadcast_to(own[:, t : t + 1], shape)
            wide[KP * k + t] = entry * scale
        wide[KP * k + k] = target(k) * scale

    def sweep(_, xs):
        xs = list(xs)
        for k in range(KP):
            terms = [wide[KP * k + t] * xs[t] for t in range(KP) if t != k]
            last = terms.pop(k - 1 if k else KP - 2)
            rest = wide[KP * k + k] - tree_sum(terms)
            xs[k] = jnp.maximum(rest - last, 0.0)
        return tuple(xs)

    xs = tuple(x_ref[8 * k : 8 * k + 8, :] for k in range(KP))
    for sweep_index in range(SWEEPS):
        xs = sweep(sweep_index, xs)
    for k in range(KP):
        new_ref[8 * k : 8 * k + 8, :] = xs[k]


def hals_traces_kernel(counts_ref, got_ref, x_ref, out_ref, new_ref, rows, grams, wide):
    counts = spread(counts_ref)
    total = tree_sum([got_ref[j] for j in range(got_ref.shape[0])])
    unpack = unpacker(counts)
    gram = total[LIVE:]
    gram = jnp.concatenate([gram[:, :LIVE], gram[:, LIVE:]], axis=0)
    rows[...] = choose_rows(unpack, total[:LIVE])
    grams[:, :KP] = choose_cols(unpack, gram)
    hals(lambda k: rows[8 * k : 8 * k + 8, :], lambda k: grams[8 * k : 8 * k + 8, :KP], x_ref, new_ref, wide)
    out_ref[...] = choose_rows(packer(counts), new_ref[...])


def hals_footprints_kernel(counts_ref, got_ref, x_ref, send_ref, new_ref, rows, grams, wide):
    counts = spread(counts_ref)
    total = tree_sum([got_ref[j] for j in range(got_ref.shape[0])])
    unpack = unpacker(counts)
    size = total.shape[0] - GRAM
    cols = jnp.concatenate([total[:size, :LIVE], total[:size, LIVE:]], axis=0)
    gram = total[size:]
    gram = jnp.concatenate([gram[:, :LIVE], gram[:, LIVE:]], axis=0)
    rows[:, : 2 * size] = choose_cols(unpack, cols)
    rows[:, 2 * size :] = jnp.zeros((KP * NP, 128 - 2 * size), F32)
    grams[:, :KP] = choose_cols(unpack, gram)
    hals(lambda k: rows[8 * k : 8 * k + 8, :], lambda k: grams[8 * k : 8 * k + 8, :KP], x_ref, new_ref, wide)
    packed = choose_rows(packer(counts), new_ref[...]).T
    chunk = jnp.concatenate([packed[:size], packed[size : 2 * size]], axis=1)
    for j in range(send_ref.shape[0]):
        send_ref[j] = chunk


def last_kernel(counts_ref, neuron_ref, all_a_ref, all_c_ref, traces_ref, foot_ref, out_ref):
    counts = spread(counts_ref)
    shape = (LIVE, KP * NP)
    patch, slot = patch_and_slot(counts, shape, 0)
    kept = (iota(shape, 1) == patch * KP + slot).astype(BF16)
    place = nt(neuron_slots(neuron_ref[...]), kept)
    live = jnp.sum(place, axis=1, keepdims=True) > 0.5
    for h in range(2):
        at = slice(128 * h, 128 * h + 128)
        out_ref[:, at] = jnp.where(live, choose_rows(place, all_c_ref[h]), traces_ref[:, at])
    half = all_a_ref.shape[0]
    unpack = unpacker(counts)
    all_a = all_a_ref[...]
    foot_ref[:, :half] = choose_cols(unpack, all_a[:, :LIVE])
    foot_ref[:, half:] = choose_cols(unpack, all_a[:, LIVE:])


def call(kernel, outs, specs, args, scratch=(), grant=32):
    return pl.pallas_call(
        kernel,
        out_shape=[jax.ShapeDtypeStruct(s, F32) for s in outs],
        in_specs=specs + [VMEM] * (len(args) - len(specs)),
        out_specs=[VMEM] * len(outs),
        scratch_shapes=list(scratch),
        compiler_params=pltpu.CompilerParams(vmem_limit_bytes=int(grant * 1024 * 1024)),
    )(*args)


def local(sizes, movie, footprints, traces, patch_counts, slot_neuron):
    n_across, n_near, n_far = sizes
    slots, patches, voxels = footprints.shape
    q = slots * patches
    foot = footprints.reshape(q, voxels)
    counts = patch_counts.reshape(1, patches)
    neuron = slot_neuron.reshape(1, q)

    def swap(x, axes):
        return lax.all_to_all(x, axes, 0, 0, tiled=True)

    def cores(x):
        return lax.all_gather(x, "core", axis=0, tiled=False)

    square = pltpu.VMEM((q, 128), F32)
    state = [(q, 128)]
    part = voxels // 2 // n_near
    for step in range(ITERS):
        halves = [(2, LIVE + GRAM, 128)]
        scratch = [square, square, pltpu.VMEM((KP * KP, NP, 128), F32)]
        if step == ITERS - 1:
            state, scratch = [], [square] + scratch
        if step == 0:
            loaded = [counts, neuron, foot, traces, movie]
            shapes = [counts.shape, neuron.shape, foot.shape, (q, traces.shape[1] // 2), movie.shape]
            buffers = [pltpu.VMEM(shape, x.dtype) for shape, x in zip(shapes, loaded)]
            buffers.append(pltpu.SemaphoreType.DMA((4 + patches,)))
            outs = halves + [(q, 128)] * 2
            partial, first_c, first_a = call(first_kernel, outs, [HBM] * 5, loaded, buffers, 53.5)
            x_c, x_a = [first_c], [first_a]
        else:
            (partial,) = call(project_kernel, halves, [], [counts, all_a, movie])
        (send,) = call(keep_half_kernel, [(n_across, LIVE + GRAM, 128)], [], [cores(partial)])
        own_c, *x_c = call(
            hals_traces_kernel, [(LIVE, 128)] + state, [], [counts, swap(send, ACROSS), *x_c], scratch
        )
        all_c = cores(own_c)
        (send,) = call(correlate_kernel, [(n_near, part + GRAM, 128)], [], [counts, all_c, movie])
        (send,) = call(keep_part_kernel, [(n_far, part + GRAM, 128)], [], [swap(send, NEAR)])
        send, *x_a = call(
            hals_footprints_kernel,
            [(n_near, part, 128)] + state,
            [],
            [counts, swap(send, FAR), *x_a],
            scratch,
        )
        all_a = swap(send, NEAR).reshape(voxels // 2, 128)
    last = [counts, neuron, all_a, all_c, traces]
    new_foot, new_traces = call(last_kernel, [foot.shape, traces.shape], [], last)
    return new_foot.reshape(footprints.shape), new_traces


def solution(mesh):
    names = ("x", "zf", "zn", "y", "core", "plane")
    shape = (2, mesh.shape["tm"] // 8, 4, mesh.shape["tile"] // 2, 2, mesh.shape["plane"])
    fine = jax.sharding.Mesh(mesh.devices.reshape(shape), names)
    frames, voxels = names[:3], names[3:]
    sizes = (shape[3] * shape[5], shape[0] * shape[2], shape[1])
    return jax.shard_map(
        functools.partial(local, sizes),
        mesh=fine,
        in_specs=(P(None, voxels, frames), P(None, None, voxels), P(None, frames), P(), P()),
        out_specs=(P(None, None, voxels), P(None, frames)),
        check_vma=False,
    )
```

```python
import functools

import jax
import jax.numpy as jnp
from jax import lax
from jax.experimental import pallas as pl
from jax.experimental.pallas import tpu as pltpu
from jax.sharding import PartitionSpec as P

ITERS = 2
SWEEPS = 3
RIDGE = 1.0
HIGH = lax.Precision.HIGHEST
F32 = jnp.float32
BF16 = jnp.bfloat16
KP = 16
NP = 8
LIVE = 64
ACROSS = ("y", "plane")
FRAMES = "tm"
GRAM = 8

def near_index(device):
    x, z = device // 16, device % 16
    a = (z + 2 * (z // 8)) % 4
    return (a // 2) * 4 + x * 2 + a % 2


def near_and_far(count):
    devices = sorted(range(count), key=lambda i: (i % 16 // 4, near_index(i)))
    near = [devices[i : i + 8] for i in range(0, count, 8)]
    return near, [list(group) for group in zip(*near)]


VMEM = pl.BlockSpec(memory_space=pltpu.VMEM)
HBM = pl.BlockSpec(memory_space=pltpu.HBM)


def nn(a, b, **kw):
    return lax.dot_general(a, b, (((1,), (0,)), ((), ())), preferred_element_type=F32, **kw)


def nt(a, b, **kw):
    return lax.dot_general(a, b, (((1,), (1,)), ((), ())), preferred_element_type=F32, **kw)


def split(x):
    high = x.astype(BF16)
    rest = x - high.astype(F32)
    middle = rest.astype(BF16)
    return [high, middle, (rest - middle.astype(F32)).astype(BF16)]


def choose_rows(pick, x):
    return nn(jnp.concatenate([pick.astype(BF16)] * 3, axis=1), jnp.concatenate(split(x), axis=0))


def choose_cols(pick, x):
    return nt(jnp.concatenate([pick.astype(BF16)] * 3, axis=1), jnp.concatenate(split(x), axis=1))


def spread(counts_ref):
    return [jnp.broadcast_to(counts_ref[:, p : p + 1], (1, 128)) for p in range(NP)]


def fit(row, shape):
    return row[:, : shape[1]] if shape[1] <= 128 else jnp.concatenate([row] * (shape[1] // 128), axis=1)


def offsets(counts, shape):
    offs = [jnp.zeros((1, 128), jnp.int32)]
    for p in range(NP - 1):
        offs.append(offs[-1] + counts[p])
    return [fit(off, shape) for off in offs]


def iota(shape, dim):
    return lax.broadcasted_iota(jnp.int32, shape, dim)


def patch_and_slot(counts, shape, dim):
    offs = offsets(counts, shape)
    r = iota(shape, dim)
    patch = jnp.zeros(shape, jnp.int32)
    slot = r
    for p in range(1, NP):
        at = r >= offs[p]
        patch = jnp.where(at, p, patch)
        slot = jnp.where(at, r - offs[p], slot)
    return patch, slot


def unpacker(counts):
    shape = (NP, LIVE)
    offs = offsets(counts, shape)
    p, r = iota(shape, 0), iota(shape, 1)
    off = jnp.zeros(shape, jnp.int32)
    cnt = jnp.zeros(shape, jnp.int32)
    for i in range(NP):
        off = jnp.where(p == i, offs[i], off)
        cnt = jnp.where(p == i, fit(counts[i], shape), cnt)
    return jnp.concatenate([((r == off + s) & (s < cnt)).astype(F32) for s in range(KP)], axis=0)


def packer(counts):
    shape = (LIVE, KP * NP)
    patch, slot = patch_and_slot(counts, shape, 0)
    return (iota(shape, 1) == slot * NP + patch).astype(F32)


def gram_chunk(counts, full):
    shape = (LIVE, LIVE)
    patch_a, _ = patch_and_slot(counts, shape, 0)
    patch_b, _ = patch_and_slot(counts, shape, 1)
    own = jnp.where(patch_a == patch_b, full, 0.0)
    _, slot = patch_and_slot(counts, (KP, LIVE), 1)
    pick = (slot == iota((KP, LIVE), 0)).astype(F32)
    by_slot = choose_rows(pick, own)
    return jnp.concatenate([by_slot[:8], by_slot[8:]], axis=1)


def project_packed(counts, packed, movie, out_ref):
    low = packed.astype(BF16)
    patch, _ = patch_and_slot(counts, low.shape, 0)
    zero = jnp.zeros_like(low)
    total = None
    for p in range(NP):
        term = nn(jnp.where(patch == p, low, zero), movie(p))
        total = term if p == 0 else total + term
    gram = gram_chunk(counts, nt(packed, packed, precision=HIGH))
    for h in range(2):
        out_ref[h, :LIVE, :] = total[:, 128 * h : 128 * h + 128]
        out_ref[h, LIVE:, :] = gram


def neuron_slots(neuron):
    shape = (KP * NP, KP * NP)
    return (iota(shape, 0) == neuron).astype(BF16)


def live_slots(counts, shape):
    q = iota(shape, 0)
    cnt = jnp.zeros(shape, jnp.int32)
    for p in range(NP):
        cnt = jnp.where(q % NP == p, counts[p], cnt)
    return q // NP < cnt


def first_traces(counts, neuron, traces_ref):
    shape = (KP * NP, KP * NP)
    q, lane = iota(shape, 0), iota(shape, 1)
    order = (lane == (q % NP) * KP + q // NP).astype(BF16)
    choose = nt(order, neuron_slots(neuron))
    half = traces_ref.shape[1] // 2
    own = traces_ref[:, pl.ds(pl.multiple_of(lax.axis_index("core") * half, half), half)]
    return jnp.where(live_slots(counts, shape), choose_rows(choose, own), 0.0)


def first_footprints(counts, foot_ref):
    lane = iota((KP * NP, 128), 1)
    half = foot_ref.shape[1] // 2
    near = near_index(lax.axis_index(FRAMES))
    base = pl.multiple_of((near // 4) * 128, 128)
    turn = 32 * (near % 4)
    first = pltpu.roll(foot_ref[:, pl.ds(base, 128)], (128 - turn) % 128, 1)
    second = pltpu.roll(foot_ref[:, pl.ds(half + base, 128)], (160 - turn) % 128, 1)
    own = jnp.where(lane < 32, first, second)
    return jnp.where(live_slots(counts, lane.shape) & (lane < 64), own, 0.0)


def first_kernel(counts_hbm, foot_hbm, movie_hbm, out_ref, counts_ref, foot_ref, movie_ref, sems):
    pairs = [(counts_hbm, counts_ref), (foot_hbm, foot_ref)]
    pairs += [(movie_hbm.at[p], movie_ref.at[p]) for p in range(NP)]
    copies = [pltpu.make_async_copy(src, dst, sems.at[i]) for i, (src, dst) in enumerate(pairs)]
    for copy in copies:
        copy.start()
    for copy in copies[:2]:
        copy.wait()
    counts = spread(counts_ref)
    packed = choose_rows(packer(counts), foot_ref[...])

    def movie(p):
        copies[2 + p].wait()
        return movie_ref[p]

    project_packed(counts, packed, movie, out_ref)


def project_kernel(counts_ref, gathered_ref, movie_ref, out_ref):
    counts = spread(counts_ref)
    rows = jnp.concatenate([gathered_ref[:128].T, gathered_ref[128:].T], axis=1)
    packed = jnp.concatenate([rows[:LIVE], rows[LIVE:]], axis=1)
    project_packed(counts, packed, lambda p: movie_ref[p], out_ref)


def keep_half_kernel(got_ref, send_ref):
    core = lax.axis_index("core")
    kept = got_ref[0, core] + got_ref[1, core]
    for j in range(send_ref.shape[0]):
        send_ref[j] = kept


def keep_part_kernel(got_ref, send_ref):
    total = tree_sum([got_ref[j] for j in range(got_ref.shape[0])])
    for j in range(send_ref.shape[0]):
        send_ref[j] = total


def correlate_kernel(counts_ref, gathered_ref, movie_ref, send_ref):
    counts = spread(counts_ref)
    rows = jnp.concatenate([gathered_ref[0], gathered_ref[1]], axis=1)
    gram = gram_chunk(counts, nt(rows, rows, precision=HIGH))
    low = rows.T.astype(BF16)
    patch, _ = patch_and_slot(counts, low.shape, 1)
    zero = jnp.zeros_like(low)
    total = None
    for p in range(NP):
        term = nn(movie_ref[p], jnp.where(patch == p, low, zero))
        total = term if p == 0 else total + term
    half = total.shape[0] // 2
    chunks = jnp.concatenate([total[:half], total[half:]], axis=1)
    n = send_ref.shape[0]
    size = half // n
    for i in range(n):
        send_ref[i, :size, :] = chunks[size * i : size * i + size]
        send_ref[i, size:, :] = gram


def tree_sum(parts):
    while len(parts) > 1:
        odd = [parts[-1]] if len(parts) % 2 else []
        parts = [a + b for a, b in zip(parts[::2], parts[1::2])] + odd
    return parts[0]


def hals(target, gram, x_ref, new_ref, wide):
    shape = (NP, 128)
    for k in range(KP):
        own = gram(k)
        scale = 1.0 / (jnp.broadcast_to(own[:, k : k + 1], shape) + RIDGE)
        for t in range(KP):
            entry = jnp.broadcast_to(own[:, t : t + 1], shape)
            wide[KP * k + t] = entry * scale
        wide[KP * k + k] = target(k) * scale

    def sweep(_, xs):
        xs = list(xs)
        for k in range(KP):
            terms = [wide[KP * k + t] * xs[t] for t in range(KP) if t != k]
            last = terms.pop(k - 1 if k else KP - 2)
            rest = wide[KP * k + k] - tree_sum(terms)
            xs[k] = jnp.maximum(rest - last, 0.0)
        return tuple(xs)

    xs = tuple(x_ref[8 * k : 8 * k + 8, :] for k in range(KP))
    for sweep_index in range(SWEEPS):
        xs = sweep(sweep_index, xs)
    for k in range(KP):
        new_ref[8 * k : 8 * k + 8, :] = xs[k]


def first_hals_traces_kernel(counts_ref, neuron_ref, traces_ref, got_ref, out_ref, new_ref, *scratch):
    new_ref[...] = first_traces(spread(counts_ref), neuron_ref[...], traces_ref)
    hals_traces_kernel(counts_ref, got_ref, new_ref, out_ref, new_ref, *scratch)


def first_hals_footprints_kernel(counts_ref, foot_ref, got_ref, send_ref, new_ref, *scratch):
    new_ref[...] = first_footprints(spread(counts_ref), foot_ref)
    hals_footprints_kernel(counts_ref, got_ref, new_ref, send_ref, new_ref, *scratch)


def hals_traces_kernel(counts_ref, got_ref, x_ref, out_ref, new_ref, rows, grams, wide):
    counts = spread(counts_ref)
    total = tree_sum([got_ref[j] for j in range(got_ref.shape[0])])
    unpack = unpacker(counts)
    gram = total[LIVE:]
    gram = jnp.concatenate([gram[:, :LIVE], gram[:, LIVE:]], axis=0)
    rows[...] = choose_rows(unpack, total[:LIVE])
    grams[:, :KP] = choose_cols(unpack, gram)
    hals(lambda k: rows[8 * k : 8 * k + 8, :], lambda k: grams[8 * k : 8 * k + 8, :KP], x_ref, new_ref, wide)
    out_ref[...] = choose_rows(packer(counts), new_ref[...])


def hals_footprints_kernel(counts_ref, got_ref, x_ref, send_ref, new_ref, rows, grams, wide):
    counts = spread(counts_ref)
    total = tree_sum([got_ref[j] for j in range(got_ref.shape[0])])
    unpack = unpacker(counts)
    size = total.shape[0] - GRAM
    cols = jnp.concatenate([total[:size, :LIVE], total[:size, LIVE:]], axis=0)
    gram = total[size:]
    gram = jnp.concatenate([gram[:, :LIVE], gram[:, LIVE:]], axis=0)
    rows[:, : 2 * size] = choose_cols(unpack, cols)
    rows[:, 2 * size :] = jnp.zeros((KP * NP, 128 - 2 * size), F32)
    grams[:, :KP] = choose_cols(unpack, gram)
    hals(lambda k: rows[8 * k : 8 * k + 8, :], lambda k: grams[8 * k : 8 * k + 8, :KP], x_ref, new_ref, wide)
    packed = choose_rows(packer(counts), new_ref[...]).T
    chunk = jnp.concatenate([packed[:size], packed[size : 2 * size]], axis=1)
    for j in range(send_ref.shape[0]):
        send_ref[j] = chunk


def last_kernel(counts_ref, neuron_ref, all_a_ref, all_c_ref, traces_ref, foot_ref, out_ref):
    counts = spread(counts_ref)
    shape = (LIVE, KP * NP)
    patch, slot = patch_and_slot(counts, shape, 0)
    kept = (iota(shape, 1) == patch * KP + slot).astype(BF16)
    place = nt(neuron_slots(neuron_ref[...]), kept)
    live = jnp.sum(place, axis=1, keepdims=True) > 0.5
    for h in range(2):
        at = slice(128 * h, 128 * h + 128)
        out_ref[:, at] = jnp.where(live, choose_rows(place, all_c_ref[h]), traces_ref[:, at])
    half = all_a_ref.shape[0]
    unpack = unpacker(counts)
    all_a = all_a_ref[...]
    foot_ref[:, :half] = choose_cols(unpack, all_a[:, :LIVE])
    foot_ref[:, half:] = choose_cols(unpack, all_a[:, LIVE:])


def call(kernel, outs, specs, args, scratch=(), grant=32):
    return pl.pallas_call(
        kernel,
        out_shape=[jax.ShapeDtypeStruct(s, F32) for s in outs],
        in_specs=specs + [VMEM] * (len(args) - len(specs)),
        out_specs=[VMEM] * len(outs),
        scratch_shapes=list(scratch),
        compiler_params=pltpu.CompilerParams(vmem_limit_bytes=int(grant * 1024 * 1024)),
    )(*args)


def local(n_across, groups, movie, footprints, traces, patch_counts, slot_neuron):
    near, far = groups
    n_near, n_far = len(near[0]), len(far[0])
    slots, patches, voxels = footprints.shape
    q = slots * patches
    foot = footprints.reshape(q, voxels)
    counts = patch_counts.reshape(1, patches)
    neuron = slot_neuron.reshape(1, q)

    def swap(x, axes, members=None):
        return lax.all_to_all(x, axes, 0, 0, tiled=True, axis_index_groups=members)

    def cores(x):
        return lax.all_gather(x, "core", axis=0, tiled=False)

    square = pltpu.VMEM((q, 128), F32)
    scratch = [square, square, pltpu.VMEM((KP * KP, NP, 128), F32)]
    part = voxels // 2 // n_near
    half = (LIVE + GRAM, 128)
    for step in range(ITERS):
        if step == 0:
            loaded = [counts, foot, movie]
            buffers = [pltpu.VMEM(x.shape, x.dtype) for x in loaded]
            buffers.append(pltpu.SemaphoreType.DMA((2 + patches,)))
            (partial,) = call(first_kernel, [(2, *half)], [HBM] * 3, loaded, buffers, 53.8)
        else:
            (partial,) = call(project_kernel, [(2, *half)], [], [counts, all_a, movie])
        (send,) = call(keep_half_kernel, [(n_across, *half)], [], [cores(partial)])
        got = swap(send, ACROSS)
        if step == 0:
            args = [counts, neuron, traces, got]
            own_c, x_c = call(first_hals_traces_kernel, [(LIVE, 128), (q, 128)], [], args, scratch)
        else:
            (own_c,) = call(hals_traces_kernel, [(LIVE, 128)], [], [counts, got, x_c], [square] + scratch)
        all_c = cores(own_c)
        (send,) = call(correlate_kernel, [(n_near, part + GRAM, 128)], [], [counts, all_c, movie])
        (send,) = call(keep_part_kernel, [(n_far, part + GRAM, 128)], [], [swap(send, FRAMES, near)])
        got = swap(send, FRAMES, far)
        if step == 0:
            args = [counts, foot, got]
            send, x_a = call(first_hals_footprints_kernel, [(n_near, part, 128), (q, 128)], [], args, scratch)
        else:
            args = [counts, got, x_a]
            (send,) = call(hals_footprints_kernel, [(n_near, part, 128)], [], args, [square] + scratch)
        all_a = swap(send, FRAMES, near).reshape(voxels // 2, 128)
    last = [counts, neuron, all_a, all_c, traces]
    new_foot, new_traces = call(last_kernel, [foot.shape, traces.shape], [], last)
    return new_foot.reshape(footprints.shape), new_traces


def solution(mesh):
    names = (FRAMES, "y", "core", "plane")
    shape = (mesh.shape["tm"], mesh.shape["tile"] // 2, 2, mesh.shape["plane"])
    fine = jax.sharding.Mesh(mesh.devices.reshape(shape), names)
    frames, voxels = FRAMES, names[1:]
    return jax.shard_map(
        functools.partial(local, shape[1] * shape[3], near_and_far(shape[0])),
        mesh=fine,
        in_specs=(P(None, voxels, frames), P(None, None, voxels), P(None, frames), P(), P()),
        out_specs=(P(None, None, voxels), P(None, frames)),
        check_vma=False,
    )
```

```python
import functools

import jax
import jax.numpy as jnp
from jax import lax
from jax.experimental import pallas as pl
from jax.experimental.pallas import tpu as pltpu
from jax.sharding import PartitionSpec as P

ITERS = 2
SWEEPS = 3
RIDGE = 1.0
HIGH = lax.Precision.HIGHEST
F32 = jnp.float32
BF16 = jnp.bfloat16
KP = 16
NP = 8
LIVE = 64
ACROSS = ("y", "plane")
FRAMES = "tm"
GRAM = 8

def near_index(device):
    x, z = device // 16, device % 16
    a = (z + 2 * (z // 8)) % 4
    return a * 2 + x


def near_and_far(count):
    devices = sorted(range(count), key=lambda i: (i % 16 // 4, near_index(i)))
    near = [devices[i : i + 8] for i in range(0, count, 8)]
    return near, [[g[0], g[2], g[1], g[3]] for g in zip(*near)]


VMEM = pl.BlockSpec(memory_space=pltpu.VMEM)
HBM = pl.BlockSpec(memory_space=pltpu.HBM)


def nn(a, b, **kw):
    return lax.dot_general(a, b, (((1,), (0,)), ((), ())), preferred_element_type=F32, **kw)


def nt(a, b, **kw):
    return lax.dot_general(a, b, (((1,), (1,)), ((), ())), preferred_element_type=F32, **kw)


def split(x):
    high = x.astype(BF16)
    rest = x - high.astype(F32)
    middle = rest.astype(BF16)
    return [high, middle, (rest - middle.astype(F32)).astype(BF16)]


def choose_rows(pick, x):
    return nn(jnp.concatenate([pick.astype(BF16)] * 3, axis=1), jnp.concatenate(split(x), axis=0))


def choose_cols(pick, x):
    return nt(jnp.concatenate([pick.astype(BF16)] * 3, axis=1), jnp.concatenate(split(x), axis=1))


def spread(counts_ref):
    return [jnp.broadcast_to(counts_ref[:, p : p + 1], (1, 128)) for p in range(NP)]


def fit(row, shape):
    return row[:, : shape[1]] if shape[1] <= 128 else jnp.concatenate([row] * (shape[1] // 128), axis=1)


def offsets(counts, shape):
    offs = [jnp.zeros((1, 128), jnp.int32)]
    for p in range(NP - 1):
        offs.append(offs[-1] + counts[p])
    return [fit(off, shape) for off in offs]


def iota(shape, dim):
    return lax.broadcasted_iota(jnp.int32, shape, dim)


def patch_and_slot(counts, shape, dim):
    offs = offsets(counts, shape)
    r = iota(shape, dim)
    patch = jnp.zeros(shape, jnp.int32)
    slot = r
    for p in range(1, NP):
        at = r >= offs[p]
        patch = jnp.where(at, p, patch)
        slot = jnp.where(at, r - offs[p], slot)
    return patch, slot


def unpacker(counts):
    shape = (NP, LIVE)
    offs = offsets(counts, shape)
    p, r = iota(shape, 0), iota(shape, 1)
    off = jnp.zeros(shape, jnp.int32)
    cnt = jnp.zeros(shape, jnp.int32)
    for i in range(NP):
        off = jnp.where(p == i, offs[i], off)
        cnt = jnp.where(p == i, fit(counts[i], shape), cnt)
    return jnp.concatenate([((r == off + s) & (s < cnt)).astype(F32) for s in range(KP)], axis=0)


def packer(counts):
    shape = (LIVE, KP * NP)
    patch, slot = patch_and_slot(counts, shape, 0)
    return (iota(shape, 1) == slot * NP + patch).astype(F32)


def gram_chunk(counts, full):
    shape = (LIVE, LIVE)
    patch_a, _ = patch_and_slot(counts, shape, 0)
    patch_b, _ = patch_and_slot(counts, shape, 1)
    own = jnp.where(patch_a == patch_b, full, 0.0)
    _, slot = patch_and_slot(counts, (KP, LIVE), 1)
    pick = (slot == iota((KP, LIVE), 0)).astype(F32)
    by_slot = choose_rows(pick, own)
    return jnp.concatenate([by_slot[:8], by_slot[8:]], axis=1)


def project_packed(counts, packed, movie):
    low = packed.astype(BF16)
    patch, _ = patch_and_slot(counts, low.shape, 0)
    zero = jnp.zeros_like(low)
    total = None
    for p in range(NP):
        term = nn(jnp.where(patch == p, low, zero), movie(p))
        total = term if p == 0 else total + term
    gram = gram_chunk(counts, nt(packed, packed, precision=HIGH))
    return [total[:, :128], total[:, 128:]], gram


def neuron_slots(neuron):
    shape = (KP * NP, KP * NP)
    return (iota(shape, 0) == neuron).astype(BF16)


def live_slots(counts, shape):
    q = iota(shape, 0)
    cnt = jnp.zeros(shape, jnp.int32)
    for p in range(NP):
        cnt = jnp.where(q % NP == p, fit(counts[p], shape), cnt)
    return q // NP < cnt


def first_traces(counts, neuron, traces):
    shape = (KP * NP, KP * NP)
    q, lane = iota(shape, 0), iota(shape, 1)
    order = (lane == (q % NP) * KP + q // NP).astype(BF16)
    choose = nt(order, neuron_slots(neuron))
    return jnp.where(live_slots(counts, traces.shape), choose_rows(choose, traces), 0.0)


def first_footprints(counts, foot_ref):
    lane = iota((KP * NP, 128), 1)
    half = foot_ref.shape[1] // 2
    near = near_index(lax.axis_index(FRAMES))
    base = pl.multiple_of((near // 4) * 128, 128)
    turn = 32 * (near % 4)
    first = pltpu.roll(foot_ref[:, pl.ds(base, 128)], (128 - turn) % 128, 1)
    second = pltpu.roll(foot_ref[:, pl.ds(half + base, 128)], (160 - turn) % 128, 1)
    own = jnp.where(lane < 32, first, second)
    return jnp.where(live_slots(counts, lane.shape) & (lane < 64), own, 0.0)


def first_kernel(counts_hbm, foot_hbm, movie_hbm, out_ref, counts_ref, foot_ref, movie_ref, sems):
    pairs = [(counts_hbm, counts_ref), (foot_hbm, foot_ref)]
    pairs += [(movie_hbm.at[p], movie_ref.at[p]) for p in range(NP)]
    copies = [pltpu.make_async_copy(src, dst, sems.at[i]) for i, (src, dst) in enumerate(pairs)]
    for copy in copies:
        copy.start()
    for copy in copies[:2]:
        copy.wait()
    counts = spread(counts_ref)
    packed = choose_rows(packer(counts), foot_ref[...])

    def movie(p):
        copies[2 + p].wait()
        return movie_ref[p]

    halves, gram = project_packed(counts, packed, movie)
    for h in range(2):
        out_ref[h, :LIVE, :] = halves[h]
        out_ref[h, LIVE:, :] = gram


def project_kernel(counts_ref, gathered_ref, movie_ref, out_ref):
    counts = spread(counts_ref)
    rows = jnp.concatenate([gathered_ref[:128].T, gathered_ref[128:].T], axis=1)
    packed = jnp.concatenate([rows[:LIVE], rows[LIVE:]], axis=1)
    halves, gram = project_packed(counts, packed, lambda p: movie_ref[p])
    for j in range(out_ref.shape[0]):
        for h in range(2):
            out_ref[j, LIVE * h : LIVE * h + LIVE, :] = halves[h]
        out_ref[j, 2 * LIVE :, :] = gram


def keep_half_kernel(got_ref, send_ref):
    core = lax.axis_index("core")
    kept = got_ref[0, core] + got_ref[1, core]
    for j in range(send_ref.shape[0]):
        send_ref[j] = kept


def add_kernel(got_ref, out_ref):
    out_ref[...] = tree_sum([got_ref[j] for j in range(got_ref.shape[0])])


def keep_part_kernel(got_ref, send_ref):
    total = tree_sum([got_ref[j] for j in range(got_ref.shape[0])])
    for j in range(send_ref.shape[0]):
        send_ref[j] = total


def correlate_kernel(counts_ref, rows_ref, movie_ref, send_ref):
    counts = spread(counts_ref)
    rows = rows_ref[...]
    gram = gram_chunk(counts, nt(rows, rows, precision=HIGH))
    low = rows.T.astype(BF16)
    patch, _ = patch_and_slot(counts, low.shape, 1)
    zero = jnp.zeros_like(low)
    total = None
    for p in range(NP):
        term = nn(movie_ref[p], jnp.where(patch == p, low, zero))
        total = term if p == 0 else total + term
    half = total.shape[0] // 2
    chunks = jnp.concatenate([total[:half], total[half:]], axis=1)
    n = send_ref.shape[0]
    size = half // n
    for i in range(n):
        send_ref[i, :size, :] = chunks[size * i : size * i + size]
        send_ref[i, size:, :] = gram


def tree_sum(parts):
    while len(parts) > 1:
        odd = [parts[-1]] if len(parts) % 2 else []
        parts = [a + b for a, b in zip(parts[::2], parts[1::2])] + odd
    return parts[0]


def hals(target, gram, x_ref, new_ref, wide):
    shape = (NP, 128)
    blocks = range(0, x_ref.shape[1], 128)
    for k in range(KP):
        own = gram[8 * k : 8 * k + 8, :KP]
        scale = 1.0 / (jnp.broadcast_to(own[:, k : k + 1], shape) + RIDGE)
        for t in range(KP):
            if t != k:
                wide[KP * k + t] = jnp.broadcast_to(own[:, t : t + 1], shape) * scale
        for at in blocks:
            target[8 * k : 8 * k + 8, at : at + 128] = target[8 * k : 8 * k + 8, at : at + 128] * scale
    xs = [[x_ref[8 * k : 8 * k + 8, at : at + 128] for k in range(KP)] for at in blocks]
    for _ in range(SWEEPS):
        for k in range(KP):
            weights = [wide[KP * k + t] for t in range(KP) if t != k]
            for at, x in zip(blocks, xs):
                terms = [w * x[t] for w, t in zip(weights, [t for t in range(KP) if t != k])]
                last = terms.pop(k - 1 if k else KP - 2)
                rest = target[8 * k : 8 * k + 8, at : at + 128] - tree_sum(terms)
                x[k] = jnp.maximum(rest - last, 0.0)
    for at, x in zip(blocks, xs):
        for k in range(KP):
            new_ref[8 * k : 8 * k + 8, at : at + 128] = x[k]


def first_hals_traces_kernel(counts_ref, neuron_ref, traces_ref, got_ref, out_ref, new_ref, *scratch):
    new_ref[...] = first_traces(spread(counts_ref), neuron_ref[...], traces_ref[...])
    hals_traces_kernel(counts_ref, got_ref, new_ref, out_ref, new_ref, *scratch)


def first_hals_footprints_kernel(counts_ref, foot_ref, got_ref, send_ref, new_ref, *scratch):
    new_ref[...] = first_footprints(spread(counts_ref), foot_ref)
    hals_footprints_kernel(counts_ref, got_ref, new_ref, send_ref, new_ref, *scratch)


def hals_traces_kernel(counts_ref, got_ref, x_ref, out_ref, new_ref, rows, grams, wide):
    counts = spread(counts_ref)
    if got_ref.shape[1] == LIVE + GRAM:
        halves, gram = [got_ref[0, :LIVE], got_ref[1, :LIVE]], got_ref[0, LIVE:]
    else:
        total = got_ref[0] + got_ref[1]
        halves, gram = [total[:LIVE], total[LIVE : 2 * LIVE]], total[2 * LIVE :]
    unpack = unpacker(counts)
    gram = jnp.concatenate([gram[:, :LIVE], gram[:, LIVE:]], axis=0)
    rows[...] = choose_rows(unpack, jnp.concatenate(halves, axis=1))
    grams[:, :KP] = choose_cols(unpack, gram)
    hals(rows, grams, x_ref, new_ref, wide)
    out_ref[...] = choose_rows(packer(counts), new_ref[...])


def hals_footprints_kernel(counts_ref, got_ref, x_ref, send_ref, new_ref, rows, grams, wide):
    counts = spread(counts_ref)
    total = tree_sum([got_ref[j] for j in range(got_ref.shape[0])])
    unpack = unpacker(counts)
    size = total.shape[0] - GRAM
    cols = jnp.concatenate([total[:size, :LIVE], total[:size, LIVE:]], axis=0)
    gram = total[size:]
    gram = jnp.concatenate([gram[:, :LIVE], gram[:, LIVE:]], axis=0)
    rows[:, : 2 * size] = choose_cols(unpack, cols)
    rows[:, 2 * size :] = jnp.zeros((KP * NP, 128 - 2 * size), F32)
    grams[:, :KP] = choose_cols(unpack, gram)
    hals(rows, grams, x_ref, new_ref, wide)
    packed = choose_rows(packer(counts), new_ref[...]).T
    chunk = jnp.concatenate([packed[:size], packed[size : 2 * size]], axis=1)
    for j in range(send_ref.shape[0]):
        send_ref[j] = chunk


def last_kernel(counts_ref, neuron_ref, all_a_ref, all_c_ref, traces_ref, foot_ref, out_ref):
    counts = spread(counts_ref)
    shape = (LIVE, KP * NP)
    patch, slot = patch_and_slot(counts, shape, 0)
    kept = (iota(shape, 1) == patch * KP + slot).astype(BF16)
    place = nt(neuron_slots(neuron_ref[...]), kept)
    live = jnp.sum(place, axis=1, keepdims=True) > 0.5
    out_ref[...] = jnp.where(live, choose_rows(place, all_c_ref[...]), traces_ref[...])
    half = all_a_ref.shape[0]
    unpack = unpacker(counts)
    all_a = all_a_ref[...]
    foot_ref[:, :half] = choose_cols(unpack, all_a[:, :LIVE])
    foot_ref[:, half:] = choose_cols(unpack, all_a[:, LIVE:])


def call(kernel, outs, specs, args, scratch=(), grant=32):
    return pl.pallas_call(
        kernel,
        out_shape=[jax.ShapeDtypeStruct(s, F32) for s in outs],
        in_specs=specs + [VMEM] * (len(args) - len(specs)),
        out_specs=[VMEM] * len(outs),
        scratch_shapes=list(scratch),
        compiler_params=pltpu.CompilerParams(vmem_limit_bytes=int(grant * 1024 * 1024)),
    )(*args)


def local(n_across, groups, movie, footprints, traces, patch_counts, slot_neuron):
    near, far = groups
    n_near, n_far = len(near[0]), len(far[0])
    slots, patches, voxels = footprints.shape
    q = slots * patches
    foot = footprints.reshape(q, voxels)
    counts = patch_counts.reshape(1, patches)
    neuron = slot_neuron.reshape(1, q)

    def swap(x, axes, members=None):
        return lax.all_to_all(x, axes, 0, 0, tiled=True, axis_index_groups=members)

    def hals_scratch(columns):
        return [pltpu.VMEM((q, columns), F32), pltpu.VMEM((q, 128), F32), pltpu.VMEM((KP * KP, NP, 128), F32)]

    frames = traces.shape[1]
    part = voxels // 2 // n_near
    half, whole = (LIVE + GRAM, 128), (2 * LIVE + GRAM, 128)

    def cores(x):
        return lax.all_gather(x, "core", axis=0, tiled=False)

    for step in range(ITERS):
        if step == 0:
            loaded = [counts, foot, movie]
            buffers = [pltpu.VMEM(x.shape, x.dtype) for x in loaded]
            buffers.append(pltpu.SemaphoreType.DMA((2 + patches,)))
            (both,) = call(first_kernel, [(2, *half)], [HBM] * 3, loaded, buffers, 53.8)
            (send,) = call(keep_half_kernel, [(n_across, *half)], [], [cores(both)])
        else:
            (send,) = call(project_kernel, [(n_across, *whole)], [], [counts, all_a, movie])
        (added,) = call(add_kernel, [send.shape[1:]], [], [swap(send, ACROSS)])
        got = cores(added)
        scratch = hals_scratch(frames)
        outs = [(LIVE, frames), (q, frames)]
        if step == 0:
            all_c, x_c = call(first_hals_traces_kernel, outs, [], [counts, neuron, traces, got], scratch)
        else:
            new = pltpu.VMEM((q, frames), F32)
            (all_c,) = call(hals_traces_kernel, outs[:1], [], [counts, got, x_c], [new] + scratch)
        (send,) = call(correlate_kernel, [(n_near, part + GRAM, 128)], [], [counts, all_c, movie])
        (send,) = call(keep_part_kernel, [(n_far, part + GRAM, 128)], [], [swap(send, FRAMES, near)])
        got = swap(send, FRAMES, far)
        scratch = hals_scratch(128)
        if step == 0:
            args = [counts, foot, got]
            send, x_a = call(first_hals_footprints_kernel, [(n_near, part, 128), (q, 128)], [], args, scratch)
        else:
            args = [counts, got, x_a]
            new = pltpu.VMEM((q, 128), F32)
            (send,) = call(hals_footprints_kernel, [(n_near, part, 128)], [], args, [new] + scratch)
        all_a = swap(send, FRAMES, near).reshape(voxels // 2, 128)
    last = [counts, neuron, all_a, all_c, traces]
    new_foot, new_traces = call(last_kernel, [foot.shape, traces.shape], [], last)
    return new_foot.reshape(footprints.shape), new_traces


def solution(mesh):
    names = (FRAMES, "y", "core", "plane")
    shape = (mesh.shape["tm"], mesh.shape["tile"] // 2, 2, mesh.shape["plane"])
    fine = jax.sharding.Mesh(mesh.devices.reshape(shape), names)
    frames, voxels = FRAMES, names[1:]
    return jax.shard_map(
        functools.partial(local, shape[1] * shape[3], near_and_far(shape[0])),
        mesh=fine,
        in_specs=(P(None, voxels, frames), P(None, None, voxels), P(None, frames), P(), P()),
        out_specs=(P(None, None, voxels), P(None, frames)),
        check_vma=False,
    )
```

```python
import functools

import jax
import jax.numpy as jnp
from jax import lax
from jax.experimental import pallas as pl
from jax.experimental.pallas import tpu as pltpu
from jax.sharding import PartitionSpec as P

ITERS = 2
SWEEPS = 3
RIDGE = 1.0
F32 = jnp.float32
BF16 = jnp.bfloat16
KP = 16
NP = 8
LIVE = 64
VOXELS = ("y", "core", "plane")
ACROSS = [(0, 0), (2, 1), (1, 0), (3, 1), (2, 0), (0, 1), (3, 0), (1, 1)]
FRAMES = "tm"
GRAM = 8

def near_index(device):
    x, z = device // 16, device % 16
    a = (z + 2 * (z // 8)) % 4
    return a * 2 + x


def near_and_far(count):
    devices = sorted(range(count), key=lambda i: (i % 16 // 4, near_index(i)))
    near = [devices[i : i + 8] for i in range(0, count, 8)]
    return near, [[g[0], g[2], g[1], g[3]] for g in zip(*near)]


VMEM = pl.BlockSpec(memory_space=pltpu.VMEM)
HBM = pl.BlockSpec(memory_space=pltpu.HBM)


def nn(a, b, **kw):
    return lax.dot_general(a, b, (((1,), (0,)), ((), ())), preferred_element_type=F32, **kw)


def nt(a, b, **kw):
    return lax.dot_general(a, b, (((1,), (1,)), ((), ())), preferred_element_type=F32, **kw)


def split(x):
    high = x.astype(BF16)
    rest = x - high.astype(F32)
    middle = rest.astype(BF16)
    return [high, middle, (rest - middle.astype(F32)).astype(BF16)]


def choose_rows(pick, x):
    return nn(jnp.concatenate([pick.astype(BF16)] * 3, axis=1), jnp.concatenate(split(x), axis=0))


def choose_cols(pick, x):
    return nt(jnp.concatenate([pick.astype(BF16)] * 3, axis=1), jnp.concatenate(split(x), axis=1))


def spread(counts_ref):
    return [jnp.broadcast_to(counts_ref[:, p : p + 1], (1, 128)) for p in range(NP)]


def fit(row, shape):
    return row[:, : shape[1]] if shape[1] <= 128 else jnp.concatenate([row] * (shape[1] // 128), axis=1)


def products(rows):
    high, low, _ = split(rows)
    return nt(jnp.concatenate([high, low, high], axis=1), jnp.concatenate([high, high, low], axis=1))


def offsets(counts, shape):
    offs = [jnp.zeros((1, 128), jnp.int32)]
    for p in range(NP - 1):
        offs.append(offs[-1] + counts[p])
    return [fit(off, shape) for off in offs]


def iota(shape, dim):
    return lax.broadcasted_iota(jnp.int32, shape, dim)


def patch_and_slot(counts, shape, dim):
    offs = offsets(counts, shape)
    r = iota(shape, dim)
    patch = jnp.zeros(shape, jnp.int32)
    slot = r
    for p in range(1, NP):
        at = r >= offs[p]
        patch = jnp.where(at, p, patch)
        slot = jnp.where(at, r - offs[p], slot)
    return patch, slot


def unpacker(counts):
    shape = (NP, LIVE)
    offs = offsets(counts, shape)
    p, r = iota(shape, 0), iota(shape, 1)
    off = jnp.zeros(shape, jnp.int32)
    cnt = jnp.zeros(shape, jnp.int32)
    for i in range(NP):
        off = jnp.where(p == i, offs[i], off)
        cnt = jnp.where(p == i, fit(counts[i], shape), cnt)
    return jnp.concatenate([((r == off + s) & (s < cnt)).astype(F32) for s in range(KP)], axis=0)


def packer(counts):
    shape = (LIVE, KP * NP)
    patch, slot = patch_and_slot(counts, shape, 0)
    return (iota(shape, 1) == slot * NP + patch).astype(F32)


def gram_chunk(counts, full):
    shape = (LIVE, LIVE)
    patch_a, _ = patch_and_slot(counts, shape, 0)
    patch_b, _ = patch_and_slot(counts, shape, 1)
    own = jnp.where(patch_a == patch_b, full, 0.0)
    _, slot = patch_and_slot(counts, (KP, LIVE), 1)
    pick = (slot == iota((KP, LIVE), 0)).astype(F32)
    by_slot = choose_rows(pick, own)
    return jnp.concatenate([by_slot[:8], by_slot[8:]], axis=1)


def project_packed(counts, packed, movie):
    low = packed.astype(BF16)
    patch, _ = patch_and_slot(counts, low.shape, 0)
    zero = jnp.zeros_like(low)
    total = None
    for p in range(NP):
        term = nn(jnp.where(patch == p, low, zero), movie(p))
        total = term if p == 0 else total + term
    gram = gram_chunk(counts, products(packed))
    return [total[:, :128], total[:, 128:]], gram


def neuron_slots(neuron):
    shape = (KP * NP, KP * NP)
    return (iota(shape, 0) == neuron).astype(BF16)


def live_slots(counts, shape):
    q = iota(shape, 0)
    cnt = jnp.zeros(shape, jnp.int32)
    for p in range(NP):
        cnt = jnp.where(q % NP == p, fit(counts[p], shape), cnt)
    return q // NP < cnt


def first_traces(counts, neuron, traces):
    shape = (KP * NP, KP * NP)
    q, lane = iota(shape, 0), iota(shape, 1)
    order = (lane == (q % NP) * KP + q // NP).astype(BF16)
    choose = nt(order, neuron_slots(neuron))
    return jnp.where(live_slots(counts, traces.shape), choose_rows(choose, traces), 0.0)


def first_footprints(counts, foot_ref):
    lane = iota((KP * NP, 128), 1)
    half = foot_ref.shape[1] // 2
    near = near_index(lax.axis_index(FRAMES))
    base = pl.multiple_of((near // 4) * 128, 128)
    turn = 32 * (near % 4)
    first = pltpu.roll(foot_ref[:, pl.ds(base, 128)], (128 - turn) % 128, 1)
    second = pltpu.roll(foot_ref[:, pl.ds(half + base, 128)], (160 - turn) % 128, 1)
    own = jnp.where(lane < 32, first, second)
    return jnp.where(live_slots(counts, lane.shape) & (lane < 64), own, 0.0)


def first_kernel(counts_hbm, foot_hbm, movie_hbm, out_ref, counts_ref, foot_ref, movie_ref, sems):
    pairs = [(counts_hbm, counts_ref), (foot_hbm, foot_ref)]
    pairs += [(movie_hbm.at[p], movie_ref.at[p]) for p in range(NP)]
    copies = [pltpu.make_async_copy(src, dst, sems.at[i]) for i, (src, dst) in enumerate(pairs)]
    for copy in copies:
        copy.start()
    for copy in copies[:2]:
        copy.wait()
    counts = spread(counts_ref)
    packed = choose_rows(packer(counts), foot_ref[...])

    def movie(p):
        copies[2 + p].wait()
        return movie_ref[p]

    halves, gram = project_packed(counts, packed, movie)
    for h in range(2):
        out_ref[h, :LIVE, :] = halves[h]
        out_ref[h, LIVE:, :] = gram


def project_kernel(counts_ref, gathered_ref, movie_ref, out_ref):
    counts = spread(counts_ref)
    rows = jnp.concatenate([gathered_ref[:128].T, gathered_ref[128:].T], axis=1)
    packed = jnp.concatenate([rows[:LIVE], rows[LIVE:]], axis=1)
    halves, gram = project_packed(counts, packed, lambda p: movie_ref[p])
    for j in range(out_ref.shape[0]):
        for h in range(2):
            out_ref[j, LIVE * h : LIVE * h + LIVE, :] = halves[h]
        out_ref[j, 2 * LIVE :, :] = gram


def keep_half_kernel(got_ref, send_ref):
    core = lax.axis_index("core")
    kept = got_ref[0, core] + got_ref[1, core]
    for j in range(send_ref.shape[0]):
        send_ref[j] = kept


def add_kernel(got_ref, out_ref):
    out_ref[...] = tree_sum([got_ref[j] for j in range(got_ref.shape[0])])


def keep_part_kernel(got_ref, send_ref):
    total = tree_sum([got_ref[j] for j in range(got_ref.shape[0])])
    for j in range(send_ref.shape[0]):
        send_ref[j] = total


def correlate_kernel(counts_ref, rows_ref, movie_ref, send_ref):
    counts = spread(counts_ref)
    rows = rows_ref[...]
    gram = gram_chunk(counts, products(rows))
    low = rows.T.astype(BF16)
    patch, _ = patch_and_slot(counts, low.shape, 1)
    zero = jnp.zeros_like(low)
    total = None
    for p in range(NP):
        term = nn(movie_ref[p], jnp.where(patch == p, low, zero))
        total = term if p == 0 else total + term
    half = total.shape[0] // 2
    chunks = jnp.concatenate([total[:half], total[half:]], axis=1)
    n = send_ref.shape[0]
    size = half // n
    for i in range(n):
        send_ref[i, :size, :] = chunks[size * i : size * i + size]
        send_ref[i, size:, :] = gram


def tree_sum(parts):
    while len(parts) > 1:
        odd = [parts[-1]] if len(parts) % 2 else []
        parts = [a + b for a, b in zip(parts[::2], parts[1::2])] + odd
    return parts[0]


def hals(target, gram, x_ref, new_ref, wide):
    shape = (NP, 128)
    blocks = range(0, x_ref.shape[1], 128)
    for k in range(KP):
        own = gram[8 * k : 8 * k + 8, :KP]
        scale = 1.0 / (jnp.broadcast_to(own[:, k : k + 1], shape) + RIDGE)
        for t in range(KP):
            if t != k:
                wide[KP * k + t] = jnp.broadcast_to(own[:, t : t + 1], shape) * scale
        for at in blocks:
            target[8 * k : 8 * k + 8, at : at + 128] = target[8 * k : 8 * k + 8, at : at + 128] * scale
    xs = [[x_ref[8 * k : 8 * k + 8, at : at + 128] for k in range(KP)] for at in blocks]
    for _ in range(SWEEPS):
        for k in range(KP):
            weights = [wide[KP * k + t] for t in range(KP) if t != k]
            for at, x in zip(blocks, xs):
                terms = [w * x[t] for w, t in zip(weights, [t for t in range(KP) if t != k])]
                last = terms.pop(k - 1 if k else KP - 2)
                rest = target[8 * k : 8 * k + 8, at : at + 128] - tree_sum(terms)
                x[k] = jnp.maximum(rest - last, 0.0)
    for at, x in zip(blocks, xs):
        for k in range(KP):
            new_ref[8 * k : 8 * k + 8, at : at + 128] = x[k]


def first_hals_traces_kernel(counts_ref, neuron_ref, traces_ref, got_ref, out_ref, new_ref, *scratch):
    new_ref[...] = first_traces(spread(counts_ref), neuron_ref[...], traces_ref[...])
    hals_traces_kernel(counts_ref, got_ref, new_ref, out_ref, new_ref, *scratch)


def first_hals_footprints_kernel(counts_ref, foot_ref, got_ref, send_ref, new_ref, *scratch):
    new_ref[...] = first_footprints(spread(counts_ref), foot_ref)
    hals_footprints_kernel(counts_ref, got_ref, new_ref, send_ref, new_ref, *scratch)


def hals_traces_kernel(counts_ref, got_ref, x_ref, out_ref, new_ref, rows, grams, wide):
    counts = spread(counts_ref)
    if got_ref.shape[1] == LIVE + GRAM:
        halves, gram = [got_ref[0, :LIVE], got_ref[1, :LIVE]], got_ref[0, LIVE:]
    else:
        total = got_ref[0] + got_ref[1]
        halves, gram = [total[:LIVE], total[LIVE : 2 * LIVE]], total[2 * LIVE :]
    unpack = unpacker(counts)
    gram = jnp.concatenate([gram[:, :LIVE], gram[:, LIVE:]], axis=0)
    rows[...] = choose_rows(unpack, jnp.concatenate(halves, axis=1))
    grams[:, :KP] = choose_cols(unpack, gram)
    hals(rows, grams, x_ref, new_ref, wide)
    out_ref[...] = choose_rows(packer(counts), new_ref[...])


def hals_footprints_kernel(counts_ref, got_ref, x_ref, send_ref, new_ref, rows, grams, wide):
    counts = spread(counts_ref)
    total = tree_sum([got_ref[j] for j in range(got_ref.shape[0])])
    unpack = unpacker(counts)
    size = total.shape[0] - GRAM
    cols = jnp.concatenate([total[:size, :LIVE], total[:size, LIVE:]], axis=0)
    gram = total[size:]
    gram = jnp.concatenate([gram[:, :LIVE], gram[:, LIVE:]], axis=0)
    rows[:, : 2 * size] = choose_cols(unpack, cols)
    rows[:, 2 * size :] = jnp.zeros((KP * NP, 128 - 2 * size), F32)
    grams[:, :KP] = choose_cols(unpack, gram)
    hals(rows, grams, x_ref, new_ref, wide)
    packed = choose_rows(packer(counts), new_ref[...]).T
    chunk = jnp.concatenate([packed[:size], packed[size : 2 * size]], axis=1)
    for j in range(send_ref.shape[0]):
        send_ref[j] = chunk


def last_kernel(counts_ref, neuron_ref, all_a_ref, all_c_ref, traces_ref, foot_ref, out_ref):
    counts = spread(counts_ref)
    shape = (LIVE, KP * NP)
    patch, slot = patch_and_slot(counts, shape, 0)
    kept = (iota(shape, 1) == patch * KP + slot).astype(BF16)
    place = nt(neuron_slots(neuron_ref[...]), kept)
    live = jnp.sum(place, axis=1, keepdims=True) > 0.5
    out_ref[...] = jnp.where(live, choose_rows(place, all_c_ref[...]), traces_ref[...])
    half = all_a_ref.shape[0]
    unpack = unpacker(counts)
    all_a = all_a_ref[...]
    foot_ref[:, :half] = choose_cols(unpack, all_a[:, :LIVE])
    foot_ref[:, half:] = choose_cols(unpack, all_a[:, LIVE:])


def call(kernel, outs, specs, args, scratch=(), grant=32):
    return pl.pallas_call(
        kernel,
        out_shape=[jax.ShapeDtypeStruct(s, F32) for s in outs],
        in_specs=specs + [VMEM] * (len(args) - len(specs)),
        out_specs=[VMEM] * len(outs),
        scratch_shapes=list(scratch),
        compiler_params=pltpu.CompilerParams(vmem_limit_bytes=int(grant * 1024 * 1024)),
    )(*args)


def local(n_across, groups, movie, footprints, traces, patch_counts, slot_neuron):
    near, far = groups
    across = [[4 * y + 2 * core + p for y, p in ACROSS] for core in range(2)]
    n_near, n_far = len(near[0]), len(far[0])
    slots, patches, voxels = footprints.shape
    q = slots * patches
    foot = footprints.reshape(q, voxels)
    counts = patch_counts.reshape(1, patches)
    neuron = slot_neuron.reshape(1, q)

    def swap(x, axes, members=None):
        return lax.all_to_all(x, axes, 0, 0, tiled=True, axis_index_groups=members)

    def hals_scratch(columns):
        return [pltpu.VMEM((q, columns), F32), pltpu.VMEM((q, 128), F32), pltpu.VMEM((KP * KP, NP, 128), F32)]

    frames = traces.shape[1]
    part = voxels // 2 // n_near
    half, whole = (LIVE + GRAM, 128), (2 * LIVE + GRAM, 128)

    def cores(x):
        return lax.all_gather(x, "core", axis=0, tiled=False)

    for step in range(ITERS):
        if step == 0:
            loaded = [counts, foot, movie]
            buffers = [pltpu.VMEM(x.shape, x.dtype) for x in loaded]
            buffers.append(pltpu.SemaphoreType.DMA((2 + patches,)))
            (both,) = call(first_kernel, [(2, *half)], [HBM] * 3, loaded, buffers, 53.8)
            (send,) = call(keep_half_kernel, [(n_across, *half)], [], [cores(both)])
        else:
            (send,) = call(project_kernel, [(n_across, *whole)], [], [counts, all_a, movie])
        (added,) = call(add_kernel, [send.shape[1:]], [], [swap(send, VOXELS, across)])
        got = cores(added)
        scratch = hals_scratch(frames)
        outs = [(LIVE, frames), (q, frames)]
        if step == 0:
            all_c, x_c = call(first_hals_traces_kernel, outs, [], [counts, neuron, traces, got], scratch)
        else:
            new = pltpu.VMEM((q, frames), F32)
            (all_c,) = call(hals_traces_kernel, outs[:1], [], [counts, got, x_c], [new] + scratch)
        (send,) = call(correlate_kernel, [(n_near, part + GRAM, 128)], [], [counts, all_c, movie])
        (send,) = call(keep_part_kernel, [(n_far, part + GRAM, 128)], [], [swap(send, FRAMES, near)])
        got = swap(send, FRAMES, far)
        scratch = hals_scratch(128)
        if step == 0:
            args = [counts, foot, got]
            send, x_a = call(first_hals_footprints_kernel, [(n_near, part, 128), (q, 128)], [], args, scratch)
        else:
            args = [counts, got, x_a]
            new = pltpu.VMEM((q, 128), F32)
            (send,) = call(hals_footprints_kernel, [(n_near, part, 128)], [], args, [new] + scratch)
        all_a = swap(send, FRAMES, near).reshape(voxels // 2, 128)
    last = [counts, neuron, all_a, all_c, traces]
    new_foot, new_traces = call(last_kernel, [foot.shape, traces.shape], [], last)
    return new_foot.reshape(footprints.shape), new_traces


def solution(mesh):
    names = (FRAMES, "y", "core", "plane")
    shape = (mesh.shape["tm"], mesh.shape["tile"] // 2, 2, mesh.shape["plane"])
    fine = jax.sharding.Mesh(mesh.devices.reshape(shape), names)
    frames, voxels = FRAMES, names[1:]
    return jax.shard_map(
        functools.partial(local, shape[1] * shape[3], near_and_far(shape[0])),
        mesh=fine,
        in_specs=(P(None, voxels, frames), P(None, None, voxels), P(None, frames), P(), P()),
        out_specs=(P(None, None, voxels), P(None, frames)),
        check_vma=False,
    )
```

```python
import functools

import jax
import jax.numpy as jnp
from jax import lax
from jax.experimental import pallas as pl
from jax.experimental.pallas import tpu as pltpu
from jax.sharding import PartitionSpec as P

ITERS = 2
SWEEPS = 3
RIDGE = 1.0
F32 = jnp.float32
BF16 = jnp.bfloat16
KP = 16
NP = 8
LIVE = 64
VOXELS = ("y", "core", "plane")
ACROSS = [(0, 0), (2, 1), (1, 0), (3, 1), (2, 0), (0, 1), (3, 0), (1, 1)]
FRAMES = "tm"
GRAM = 8

def near_index(device):
    x, z = device // 16, device % 16
    a = (z + 2 * (z // 8)) % 4
    return a * 2 + x


def near_and_far(count):
    devices = sorted(range(count), key=lambda i: (i % 16 // 4, near_index(i)))
    near = [devices[i : i + 8] for i in range(0, count, 8)]
    return near, [[g[0], g[2], g[1], g[3]] for g in zip(*near)]


VMEM = pl.BlockSpec(memory_space=pltpu.VMEM)
HBM = pl.BlockSpec(memory_space=pltpu.HBM)


def nn(a, b, **kw):
    return lax.dot_general(a, b, (((1,), (0,)), ((), ())), preferred_element_type=F32, **kw)


def nt(a, b, **kw):
    return lax.dot_general(a, b, (((1,), (1,)), ((), ())), preferred_element_type=F32, **kw)


def split(x):
    high = x.astype(BF16)
    rest = x - high.astype(F32)
    middle = rest.astype(BF16)
    return [high, middle, (rest - middle.astype(F32)).astype(BF16)]


def choose_rows(pick, x):
    return nn(jnp.concatenate([pick.astype(BF16)] * 3, axis=1), jnp.concatenate(split(x), axis=0))


def choose_cols(pick, x):
    return nt(jnp.concatenate([pick.astype(BF16)] * 3, axis=1), jnp.concatenate(split(x), axis=1))


def spread(counts_ref):
    return [jnp.broadcast_to(counts_ref[:, p : p + 1], (1, 128)) for p in range(NP)]


def fit(row, shape):
    return row[:, : shape[1]] if shape[1] <= 128 else jnp.concatenate([row] * (shape[1] // 128), axis=1)


def products(rows):
    high, low, _ = split(rows)
    return nt(jnp.concatenate([high, low, high], axis=1), jnp.concatenate([high, high, low], axis=1))


def offsets(counts, shape):
    offs = [jnp.zeros((1, 128), jnp.int32)]
    for p in range(NP - 1):
        offs.append(offs[-1] + counts[p])
    return [fit(off, shape) for off in offs]


def iota(shape, dim):
    return lax.broadcasted_iota(jnp.int32, shape, dim)


def patch_and_slot(counts, shape, dim):
    offs = offsets(counts, shape)
    r = iota(shape, dim)
    patch = jnp.zeros(shape, jnp.int32)
    slot = r
    for p in range(1, NP):
        at = r >= offs[p]
        patch = jnp.where(at, p, patch)
        slot = jnp.where(at, r - offs[p], slot)
    return patch, slot


def unpacker(counts):
    shape = (NP, LIVE)
    offs = offsets(counts, shape)
    p, r = iota(shape, 0), iota(shape, 1)
    off = jnp.zeros(shape, jnp.int32)
    cnt = jnp.zeros(shape, jnp.int32)
    for i in range(NP):
        off = jnp.where(p == i, offs[i], off)
        cnt = jnp.where(p == i, fit(counts[i], shape), cnt)
    return jnp.concatenate([((r == off + s) & (s < cnt)).astype(F32) for s in range(KP)], axis=0)


def packer(counts):
    shape = (LIVE, KP * NP)
    patch, slot = patch_and_slot(counts, shape, 0)
    return (iota(shape, 1) == slot * NP + patch).astype(F32)


def gram_chunk(counts, full):
    shape = (LIVE, LIVE)
    patch_a, _ = patch_and_slot(counts, shape, 0)
    patch_b, _ = patch_and_slot(counts, shape, 1)
    own = jnp.where(patch_a == patch_b, full, 0.0)
    _, slot = patch_and_slot(counts, (KP, LIVE), 1)
    pick = (slot == iota((KP, LIVE), 0)).astype(F32)
    by_slot = choose_rows(pick, own)
    return jnp.concatenate([by_slot[:8], by_slot[8:]], axis=1)


def project_packed(counts, packed, movie):
    low = packed.astype(BF16)
    patch, _ = patch_and_slot(counts, low.shape, 0)
    zero = jnp.zeros_like(low)
    total = None
    for p in range(NP):
        term = nn(jnp.where(patch == p, low, zero), movie(p))
        total = term if p == 0 else total + term
    gram = gram_chunk(counts, products(packed))
    return [total[:, :128], total[:, 128:]], gram


def neuron_slots(neuron):
    shape = (KP * NP, KP * NP)
    return (iota(shape, 0) == neuron).astype(BF16)


def live_slots(counts, shape):
    q = iota(shape, 0)
    cnt = jnp.zeros(shape, jnp.int32)
    for p in range(NP):
        cnt = jnp.where(q % NP == p, fit(counts[p], shape), cnt)
    return q // NP < cnt


def first_traces(counts, neuron, traces):
    shape = (KP * NP, KP * NP)
    q, lane = iota(shape, 0), iota(shape, 1)
    order = (lane == (q % NP) * KP + q // NP).astype(BF16)
    choose = nt(order, neuron_slots(neuron))
    return jnp.where(live_slots(counts, traces.shape), choose_rows(choose, traces), 0.0)


def first_footprints(counts, foot_ref):
    lane = iota((KP * NP, 128), 1)
    half = foot_ref.shape[1] // 2
    near = near_index(lax.axis_index(FRAMES))
    base = pl.multiple_of((near // 4) * 128, 128)
    turn = 32 * (near % 4)
    first = pltpu.roll(foot_ref[:, pl.ds(base, 128)], (128 - turn) % 128, 1)
    second = pltpu.roll(foot_ref[:, pl.ds(half + base, 128)], (160 - turn) % 128, 1)
    own = jnp.where(lane < 32, first, second)
    return jnp.where(live_slots(counts, lane.shape) & (lane < 64), own, 0.0)


def first_kernel(counts_hbm, foot_hbm, movie_hbm, out_ref, counts_ref, foot_ref, movie_ref, sems):
    pairs = [(counts_hbm, counts_ref), (foot_hbm, foot_ref)]
    pairs += [(movie_hbm.at[p], movie_ref.at[p]) for p in range(NP)]
    copies = [pltpu.make_async_copy(src, dst, sems.at[i]) for i, (src, dst) in enumerate(pairs)]
    for copy in copies:
        copy.start()
    for copy in copies[:2]:
        copy.wait()
    counts = spread(counts_ref)
    packed = choose_rows(packer(counts), foot_ref[...])

    def movie(p):
        copies[2 + p].wait()
        return movie_ref[p]

    halves, gram = project_packed(counts, packed, movie)
    for h in range(2):
        out_ref[h, :LIVE, :] = halves[h]
        out_ref[h, LIVE:, :] = gram


def project_kernel(counts_ref, gathered_ref, movie_ref, out_ref):
    counts = spread(counts_ref)
    rows = jnp.concatenate([gathered_ref[:128].T, gathered_ref[128:].T], axis=1)
    packed = jnp.concatenate([rows[:LIVE], rows[LIVE:]], axis=1)
    halves, gram = project_packed(counts, packed, lambda p: movie_ref[p])
    for j in range(out_ref.shape[0]):
        for h in range(2):
            out_ref[j, LIVE * h : LIVE * h + LIVE, :] = halves[h]
        out_ref[j, 2 * LIVE :, :] = gram


def keep_half_kernel(got_ref, send_ref):
    core = lax.axis_index("core")
    kept = got_ref[0, core] + got_ref[1, core]
    for j in range(send_ref.shape[0]):
        send_ref[j] = kept


def add_kernel(got_ref, out_ref):
    out_ref[...] = tree_sum([got_ref[j] for j in range(got_ref.shape[0])])


def keep_part_kernel(got_ref, send_ref):
    total = tree_sum([got_ref[j] for j in range(got_ref.shape[0])])
    for j in range(send_ref.shape[0]):
        send_ref[j] = total


def correlate_kernel(counts_ref, rows_ref, movie_ref, send_ref):
    counts = spread(counts_ref)
    rows = rows_ref[...]
    gram = gram_chunk(counts, products(rows))
    low = rows.astype(BF16)
    patch, _ = patch_and_slot(counts, low.shape, 0)
    zero = jnp.zeros_like(low)
    total = None
    for p in range(NP):
        term = nt(movie_ref[p], jnp.where(patch == p, low, zero))
        total = term if p == 0 else total + term
    half = total.shape[0] // 2
    chunks = jnp.concatenate([total[:half], total[half:]], axis=1)
    n = send_ref.shape[0]
    size = half // n
    for i in range(n):
        send_ref[i, :size, :] = chunks[size * i : size * i + size]
        send_ref[i, size:, :] = gram


def tree_sum(parts):
    while len(parts) > 1:
        odd = [parts[-1]] if len(parts) % 2 else []
        parts = [a + b for a, b in zip(parts[::2], parts[1::2])] + odd
    return parts[0]


def hals(target, gram, x_ref, new_ref, wide):
    shape = (NP, 128)
    blocks = range(0, x_ref.shape[1], 128)
    for k in range(KP):
        own = gram[8 * k : 8 * k + 8, :KP]
        scale = 1.0 / (jnp.broadcast_to(own[:, k : k + 1], shape) + RIDGE)
        for t in range(KP):
            if t != k:
                wide[KP * k + t] = jnp.broadcast_to(own[:, t : t + 1], shape) * scale
        for at in blocks:
            target[8 * k : 8 * k + 8, at : at + 128] = target[8 * k : 8 * k + 8, at : at + 128] * scale
    xs = [[x_ref[8 * k : 8 * k + 8, at : at + 128] for k in range(KP)] for at in blocks]
    for _ in range(SWEEPS):
        for k in range(KP):
            weights = [wide[KP * k + t] for t in range(KP) if t != k]
            for at, x in zip(blocks, xs):
                terms = [w * x[t] for w, t in zip(weights, [t for t in range(KP) if t != k])]
                last = terms.pop(k - 1 if k else KP - 2)
                rest = target[8 * k : 8 * k + 8, at : at + 128] - tree_sum(terms)
                x[k] = jnp.maximum(rest - last, 0.0)
    for at, x in zip(blocks, xs):
        for k in range(KP):
            new_ref[8 * k : 8 * k + 8, at : at + 128] = x[k]


def first_hals_traces_kernel(counts_ref, neuron_ref, traces_ref, got_ref, out_ref, new_ref, *scratch):
    new_ref[...] = first_traces(spread(counts_ref), neuron_ref[...], traces_ref[...])
    hals_traces_kernel(counts_ref, got_ref, new_ref, out_ref, new_ref, *scratch)


def first_hals_footprints_kernel(counts_ref, foot_ref, got_ref, send_ref, new_ref, *scratch):
    new_ref[...] = first_footprints(spread(counts_ref), foot_ref)
    hals_footprints_kernel(counts_ref, got_ref, new_ref, send_ref, new_ref, *scratch)


def hals_traces_kernel(counts_ref, got_ref, x_ref, out_ref, new_ref, rows, grams, wide):
    counts = spread(counts_ref)
    if got_ref.shape[1] == LIVE + GRAM:
        halves, gram = [got_ref[0, :LIVE], got_ref[1, :LIVE]], got_ref[0, LIVE:]
    else:
        total = got_ref[0] + got_ref[1]
        halves, gram = [total[:LIVE], total[LIVE : 2 * LIVE]], total[2 * LIVE :]
    unpack = unpacker(counts)
    gram = jnp.concatenate([gram[:, :LIVE], gram[:, LIVE:]], axis=0)
    rows[...] = choose_rows(unpack, jnp.concatenate(halves, axis=1))
    grams[:, :KP] = choose_cols(unpack, gram)
    hals(rows, grams, x_ref, new_ref, wide)
    out_ref[...] = choose_rows(packer(counts), new_ref[...])


def hals_footprints_kernel(counts_ref, got_ref, x_ref, send_ref, new_ref, rows, grams, wide):
    counts = spread(counts_ref)
    total = tree_sum([got_ref[j] for j in range(got_ref.shape[0])])
    unpack = unpacker(counts)
    size = total.shape[0] - GRAM
    cols = jnp.concatenate([total[:size, :LIVE], total[:size, LIVE:]], axis=0)
    gram = total[size:]
    gram = jnp.concatenate([gram[:, :LIVE], gram[:, LIVE:]], axis=0)
    rows[:, : 2 * size] = choose_cols(unpack, cols)
    rows[:, 2 * size :] = jnp.zeros((KP * NP, 128 - 2 * size), F32)
    grams[:, :KP] = choose_cols(unpack, gram)
    hals(rows, grams, x_ref, new_ref, wide)
    packed = choose_rows(packer(counts), new_ref[...]).T
    chunk = jnp.concatenate([packed[:size], packed[size : 2 * size]], axis=1)
    for j in range(send_ref.shape[0]):
        send_ref[j] = chunk


def last_kernel(counts_ref, neuron_ref, all_a_ref, all_c_ref, traces_ref, foot_ref, out_ref):
    counts = spread(counts_ref)
    shape = (LIVE, KP * NP)
    patch, slot = patch_and_slot(counts, shape, 0)
    kept = (iota(shape, 1) == patch * KP + slot).astype(BF16)
    place = nt(neuron_slots(neuron_ref[...]), kept)
    live = jnp.sum(place, axis=1, keepdims=True) > 0.5
    out_ref[...] = jnp.where(live, choose_rows(place, all_c_ref[...]), traces_ref[...])
    half = all_a_ref.shape[0]
    unpack = unpacker(counts)
    all_a = all_a_ref[...]
    foot_ref[:, :half] = choose_cols(unpack, all_a[:, :LIVE])
    foot_ref[:, half:] = choose_cols(unpack, all_a[:, LIVE:])


def call(kernel, outs, specs, args, scratch=(), grant=32):
    return pl.pallas_call(
        kernel,
        out_shape=[jax.ShapeDtypeStruct(s, F32) for s in outs],
        in_specs=specs + [VMEM] * (len(args) - len(specs)),
        out_specs=[VMEM] * len(outs),
        scratch_shapes=list(scratch),
        compiler_params=pltpu.CompilerParams(vmem_limit_bytes=int(grant * 1024 * 1024)),
    )(*args)


def local(n_across, groups, movie, footprints, traces, patch_counts, slot_neuron):
    near, far = groups
    across = [[4 * y + 2 * core + p for y, p in ACROSS] for core in range(2)]
    n_near, n_far = len(near[0]), len(far[0])
    slots, patches, voxels = footprints.shape
    q = slots * patches
    foot = footprints.reshape(q, voxels)
    counts = patch_counts.reshape(1, patches)
    neuron = slot_neuron.reshape(1, q)

    def swap(x, axes, members=None):
        return lax.all_to_all(x, axes, 0, 0, tiled=True, axis_index_groups=members)

    def hals_scratch(columns):
        return [pltpu.VMEM((q, columns), F32), pltpu.VMEM((q, 128), F32), pltpu.VMEM((KP * KP, NP, 128), F32)]

    frames = traces.shape[1]
    part = voxels // 2 // n_near
    half, whole = (LIVE + GRAM, 128), (2 * LIVE + GRAM, 128)

    def cores(x):
        return lax.all_gather(x, "core", axis=0, tiled=False)

    for step in range(ITERS):
        if step == 0:
            loaded = [counts, foot, movie]
            buffers = [pltpu.VMEM(x.shape, x.dtype) for x in loaded]
            buffers.append(pltpu.SemaphoreType.DMA((2 + patches,)))
            (both,) = call(first_kernel, [(2, *half)], [HBM] * 3, loaded, buffers, 53.8)
            (send,) = call(keep_half_kernel, [(n_across, *half)], [], [cores(both)])
        else:
            (send,) = call(project_kernel, [(n_across, *whole)], [], [counts, all_a, movie])
        (added,) = call(add_kernel, [send.shape[1:]], [], [swap(send, VOXELS, across)])
        got = cores(added)
        scratch = hals_scratch(frames)
        outs = [(LIVE, frames), (q, frames)]
        if step == 0:
            all_c, x_c = call(first_hals_traces_kernel, outs, [], [counts, neuron, traces, got], scratch)
        else:
            new = pltpu.VMEM((q, frames), F32)
            (all_c,) = call(hals_traces_kernel, outs[:1], [], [counts, got, x_c], [new] + scratch)
        (send,) = call(correlate_kernel, [(n_near, part + GRAM, 128)], [], [counts, all_c, movie])
        (send,) = call(keep_part_kernel, [(n_far, part + GRAM, 128)], [], [swap(send, FRAMES, near)])
        got = swap(send, FRAMES, far)
        scratch = hals_scratch(128)
        if step == 0:
            args = [counts, foot, got]
            send, x_a = call(first_hals_footprints_kernel, [(n_near, part, 128), (q, 128)], [], args, scratch)
        else:
            args = [counts, got, x_a]
            new = pltpu.VMEM((q, 128), F32)
            (send,) = call(hals_footprints_kernel, [(n_near, part, 128)], [], args, [new] + scratch)
        all_a = swap(send, FRAMES, near).reshape(voxels // 2, 128)
    last = [counts, neuron, all_a, all_c, traces]
    new_foot, new_traces = call(last_kernel, [foot.shape, traces.shape], [], last)
    return new_foot.reshape(footprints.shape), new_traces


def solution(mesh):
    names = (FRAMES, "y", "core", "plane")
    shape = (mesh.shape["tm"], mesh.shape["tile"] // 2, 2, mesh.shape["plane"])
    fine = jax.sharding.Mesh(mesh.devices.reshape(shape), names)
    frames, voxels = FRAMES, names[1:]
    return jax.shard_map(
        functools.partial(local, shape[1] * shape[3], near_and_far(shape[0])),
        mesh=fine,
        in_specs=(P(None, voxels, frames), P(None, None, voxels), P(None, frames), P(), P()),
        out_specs=(P(None, None, voxels), P(None, frames)),
        check_vma=False,
    )
```
